512 devices in a mesh: dp: 32 (over z, x_lo, core), dap: 16 (over y, x_hi).
Axes of the slice: x: 4 (x_hi: 2, x_lo: 2; x = x_hi * 2 + x_lo), y: 8, z: 8, core: 2. Of those that a mesh axis runs over, the one named last changes fastest.
Arguments:
- pair_repr: bfloat16 [32, 128, 128, 128], P('dp', 'dap'), may hold values from -6 to 6
- cotangent: bfloat16 [32, 128, 128, 128], P('dp', None, 'dap'), may hold values from -6 to 6
- residue_mask: int32 [32, 128], P('dp'), may hold values 0 or 1
- norm_gains: float32 [3, 128], replicated, may hold values from 0.1 to 1.9
- w_proj: bfloat16 [4, 128, 128], replicated, may hold values from -0.5 to 0.5
- w_out: bfloat16 [2, 128, 128], replicated, may hold values from -0.5 to 0.5
- w_up: bfloat16 [128, 512], replicated, may hold values from -0.5 to 0.5
- w_down: bfloat16 [512, 128], replicated, may hold values from -0.25 to 0.25
Outputs:
- pair_next: bfloat16 [32, 128, 128, 128], P('dp', None, 'dap')
- pair_grad: bfloat16 [32, 128, 128, 128], P('dp', 'dap')
- grad_proj: bfloat16 [4, 128, 128], replicated
- grad_out: bfloat16 [2, 128, 128], replicated
- grad_up: bfloat16 [128, 512], replicated
- grad_down: bfloat16 [512, 128], replicated
- grad_gains: bfloat16 [3, 128], replicated
The draws below stay inside these ranges and needn't reach their ends.
Inputs may be any that keep to these rules, and one draw needn't show every extreme that they name: `residue_mask`: 1 marks a residue inside the crop, 0 padding.
All inputs are finite; a program needn't handle non-finite values. No bound on the sum of `residue_mask` on one device may be relied on, other than what follows from the above.
Results may differ from the reference program's by a relative error of at most 0.022.
Values may be sent and summed in bfloat16 or wider, within the bound.
A program may use at most 64 MiB of HBM per device.

```python
import math
import jax
import jax.numpy as jnp
from jax import lax

C = 128
FFN = 512
N = 128
BATCH = 32


def with_ends(values, key, smallest, top_value):
    extent = values.shape
    place = [jax.random.randint(jax.random.fold_in(key, axis), (), 0, extent[axis]) for axis in range(len(extent))]
    values = values.at[tuple(place)].set(smallest)
    longest = extent.index(max(extent))
    place[longest] = (place[longest] + 1) % extent[longest]
    return values.at[tuple(place)].set(top_value)


def block_levels(own_key, dims, pieces, smallest, top_value):
    loudness = 1.0
    for axis_at, blocks in pieces:
        steps = jax.random.uniform(jax.random.fold_in(jax.random.fold_in(own_key, 6), axis_at), (blocks,), jnp.float32, smallest / len(pieces), top_value / len(pieces))
        loudness = loudness * jnp.repeat(jnp.exp(steps), dims[axis_at] // blocks).reshape((-1,) + (1,) * (len(dims) - 1 - axis_at))
    return loudness


def scatter_about(stream_key, shape, deviation, limit, split=(), dtype=jnp.bfloat16):
    drawn = deviation * jax.random.normal(stream_key, shape, jnp.float32)
    if split:
        drawn = drawn * block_levels(stream_key, shape, split, -0.22, 0.18)
    return jnp.clip(drawn, -limit, limit).astype(dtype)


def setup_inputs(seed: int = 0) -> dict:
    splits = jax.random.split(jax.random.key(seed), 9)
    return {
        "pair_repr": scatter_about(splits[0], (BATCH, N, N, C), 1.0, 6.0, ((0, 32), (1, 16))),
        "cotangent": scatter_about(splits[1], (BATCH, N, N, C), 1.0, 6.0, ((0, 32), (2, 16))),
        "residue_mask": with_ends((jax.random.randint(splits[2], (BATCH, N), 0, 8) < 7).astype(jnp.int32), jax.random.fold_in(splits[2], 1), 0, 1),
        "norm_gains": jnp.clip(1.0 + 0.18 * jax.random.normal(splits[3], (3, C), jnp.float32), 0.1, 1.9),
        "w_proj": scatter_about(splits[4], (4, C, C), C ** -0.5, 0.5),
        "w_out": scatter_about(splits[5], (2, C, C), C ** -0.5, 0.5),
        "w_up": scatter_about(splits[6], (C, FFN), C ** -0.5, 0.5),
        "w_down": scatter_about(splits[7], (FFN, C), FFN ** -0.5, 0.25),
    }


EPSILON = 1e-05
GELU_SCALE = 0.7978845608028654
GELU_CUBIC = 0.044715

def normalize(values, gain_row):
    average = lax.optimization_barrier(jnp.mean(values, axis=-1, keepdims=True))
    centred = values - average
    inv_std = lax.rsqrt(lax.optimization_barrier(jnp.mean(centred * centred, axis=-1, keepdims=True)) + EPSILON)
    normed = centred * inv_std
    return (normed * gain_row, normed, inv_std)

def normalize_back(incoming, normed, inv_std, gain_row):
    scaled = incoming * gain_row
    inner_sum = scaled - lax.optimization_barrier(jnp.mean(scaled, axis=-1, keepdims=True)) - normed * lax.optimization_barrier(jnp.mean(scaled * normed, axis=-1, keepdims=True))
    return (inv_std * inner_sum, lax.optimization_barrier(jnp.sum(incoming * normed, axis=0)))

def gelu_parts(pre_act):
    tanh_value = jnp.tanh(GELU_SCALE * (pre_act + GELU_CUBIC * pre_act * pre_act * pre_act))
    activation = 0.5 * pre_act * (1.0 + tanh_value)
    slopes = 0.5 * (1.0 + tanh_value) + 0.5 * pre_act * (1.0 - tanh_value * tanh_value) * GELU_SCALE * (1.0 + 3.0 * GELU_CUBIC * pre_act * pre_act)
    return (activation, slopes)

def matmul(left_side, right_side):
    return jnp.dot(left_side, right_side, preferred_element_type=jnp.float32)

def weight_grad(inputs, outputs):
    return lax.dot_general(inputs, outputs, (((0,), (0,)), ((), ())), preferred_element_type=jnp.float32)

def front_pass(pair_rows, pair_mask, gain_rows, w_proj):
    pair_f = pair_rows.astype(jnp.float32)
    normed_out, pair_hat, pair_rstd = normalize(pair_f, gain_rows[0])
    pair_ln = normed_out.astype(jnp.bfloat16)
    a_gate = jax.nn.sigmoid(matmul(pair_ln, w_proj[0]))
    a_value = matmul(pair_ln, w_proj[1])
    b_gate = jax.nn.sigmoid(matmul(pair_ln, w_proj[2]))
    b_value = matmul(pair_ln, w_proj[3])
    left_proj = (pair_mask * a_gate * a_value).astype(jnp.bfloat16)
    right_proj = (pair_mask * b_gate * b_value).astype(jnp.bfloat16)
    stored = (pair_f, pair_ln, pair_hat, pair_rstd, a_gate, a_value, b_gate, b_value)
    return (left_proj, right_proj, stored)

def middle_pass(tri_sum, stored_front, gain_rows, w_out, w_up, w_down):
    pair_f = stored_front[0]
    pair_ln = stored_front[1]
    normed_out, tri_hat, tri_rstd = normalize(tri_sum, gain_rows[1])
    tri_ln = normed_out.astype(jnp.bfloat16)
    out_gate = jax.nn.sigmoid(matmul(pair_ln, w_out[0]))
    out_value = matmul(tri_ln, w_out[1])
    pair_mid = (pair_f + out_gate * out_value).astype(jnp.bfloat16)
    mid_f = pair_mid.astype(jnp.float32)
    normed_mid, mid_hat, mid_rstd = normalize(mid_f, gain_rows[2])
    mid_ln = normed_mid.astype(jnp.bfloat16)
    activation, slopes = gelu_parts(matmul(mid_ln, w_up))
    hidden = activation.astype(jnp.bfloat16)
    pair_out = (mid_f + matmul(hidden, w_down)).astype(jnp.bfloat16)
    stored = (tri_ln, tri_hat, tri_rstd, out_gate, out_value, mid_ln, mid_hat, mid_rstd, slopes, hidden)
    return (pair_out, stored)

def upper_back(cot_rows, stored_front, stored_mid, gain_rows, w_out, w_up, w_down):
    tri_ln, tri_hat, tri_rstd, out_gate, out_value, mid_ln, mid_hat, mid_rstd, slopes, hidden = stored_mid
    pair_ln = stored_front[1]
    grad_down = weight_grad(hidden, cot_rows)
    d_pre = (matmul(cot_rows, w_down.T) * slopes).astype(jnp.bfloat16)
    grad_up = weight_grad(mid_ln, d_pre)
    d_norm, gain_mid = normalize_back(matmul(d_pre, w_up.T), mid_hat, mid_rstd, gain_rows[2])
    d_mid = d_norm + cot_rows.astype(jnp.float32)
    d_gate = (d_mid * out_value * out_gate * (1.0 - out_gate)).astype(jnp.bfloat16)
    d_value = (d_mid * out_gate).astype(jnp.bfloat16)
    grad_gate = weight_grad(pair_ln, d_gate)
    grad_value = weight_grad(tri_ln, d_value)
    d_tri, gain_tri = normalize_back(matmul(d_value, w_out[1].T), tri_hat, tri_rstd, gain_rows[1])
    return (d_tri.astype(jnp.bfloat16), d_mid, d_gate, (grad_down, grad_up, gain_mid), (grad_gate, grad_value, gain_tri))

def lower_back(d_left, d_right, d_mid, d_gate, stored_front, pair_mask, gain_rows, w_proj, w_out):
    pair_ln = stored_front[1]
    pair_hat = stored_front[2]
    pair_rstd = stored_front[3]
    a_gate, a_value, b_gate, b_value = (stored_front[4], stored_front[5], stored_front[6], stored_front[7])
    left_masked = d_left * pair_mask
    right_masked = d_right * pair_mask
    d_ag = (left_masked * a_value * a_gate * (1.0 - a_gate)).astype(jnp.bfloat16)
    d_av = (left_masked * a_gate).astype(jnp.bfloat16)
    d_bg = (right_masked * b_value * b_gate * (1.0 - b_gate)).astype(jnp.bfloat16)
    d_bv = (right_masked * b_gate).astype(jnp.bfloat16)
    grad_proj = jnp.stack([weight_grad(pair_ln, d_ag), weight_grad(pair_ln, d_av), weight_grad(pair_ln, d_bg), weight_grad(pair_ln, d_bv)])
    d_ln = matmul(d_gate, w_out[0].T) + matmul(d_ag, w_proj[0].T) + matmul(d_av, w_proj[1].T) + matmul(d_bg, w_proj[2].T) + matmul(d_bv, w_proj[3].T)
    d_pair, gain_pair = normalize_back(d_ln, pair_hat, pair_rstd, gain_rows[0])
    return ((d_mid + d_pair).astype(jnp.bfloat16), grad_proj, gain_pair)

def reference(pair_repr, cotangent, residue_mask, norm_gains, w_proj, w_out, w_up, w_down):
    residues = pair_repr.shape[1]
    channels = pair_repr.shape[3]
    row_count = residues * residues

    def crop_step(carry, inputs):
        crop_pair, crop_cot, crop_mask = inputs
        mask_f = crop_mask.astype(jnp.float32)
        pair_mask = (mask_f[:, None] * mask_f[None, :]).reshape(row_count, 1)
        left_proj, right_proj, stored_front = front_pass(crop_pair.reshape(row_count, channels), pair_mask, norm_gains, w_proj)
        left_cube = left_proj.reshape(residues, residues, channels).astype(jnp.float32)
        right_cube = right_proj.reshape(residues, residues, channels).astype(jnp.float32)
        tri_sum = jnp.einsum('ikc,jkc->ijc', left_cube, right_cube).reshape(row_count, channels)
        pair_out, stored_mid = middle_pass(tri_sum, stored_front, norm_gains, w_out, w_up, w_down)
        d_tri, d_mid, d_gate, trans_part, tri_part = upper_back(crop_cot.reshape(row_count, channels), stored_front, stored_mid, norm_gains, w_out, w_up, w_down)
        d_cube = d_tri.reshape(residues, residues, channels).astype(jnp.float32)
        d_left = jnp.einsum('ijc,jkc->ikc', d_cube, right_cube).reshape(row_count, channels)
        d_right = jnp.einsum('ijc,ikc->jkc', d_cube, left_cube).reshape(row_count, channels)
        pair_grad, grad_proj, gain_pair = lower_back(d_left, d_right, d_mid, d_gate, stored_front, pair_mask, norm_gains, w_proj, w_out)
        grad_gains = jnp.stack([gain_pair, tri_part[2], trans_part[2]])
        carry = (carry[0] + grad_proj, carry[1] + jnp.stack([tri_part[0], tri_part[1]]), carry[2] + trans_part[1], carry[3] + trans_part[0], carry[4] + grad_gains)
        return (carry, (pair_out.reshape(residues, residues, channels), pair_grad.reshape(residues, residues, channels)))
    start_sums = (jnp.zeros(w_proj.shape, jnp.float32), jnp.zeros(w_out.shape, jnp.float32), jnp.zeros(w_up.shape, jnp.float32), jnp.zeros(w_down.shape, jnp.float32), jnp.zeros(norm_gains.shape, jnp.float32))
    sums, outputs = lax.scan(crop_step, start_sums, (pair_repr, cotangent, residue_mask))
    grad_scale = 1.0 / math.sqrt(pair_repr.shape[0] * row_count)
    return (outputs[0], outputs[1], (sums[0] * grad_scale).astype(jnp.bfloat16), (sums[1] * grad_scale).astype(jnp.bfloat16), (sums[2] * grad_scale).astype(jnp.bfloat16), (sums[3] * grad_scale).astype(jnp.bfloat16), (sums[4] * grad_scale).astype(jnp.bfloat16))
```

```python
import functools
import math

import jax
import jax.numpy as jnp
from jax import lax
from jax.experimental import pallas as pl
from jax.experimental.pallas import tpu as pltpu
from jax.sharding import PartitionSpec as P

EPSILON = 1e-05
GELU_SCALE = 0.7978845608028654
GELU_CUBIC = 0.044715
MESH = pl.DeviceIdType.MESH
F32 = jnp.float32
BF16 = jnp.bfloat16

C = 128
FFN = 512
ROWS = 8
PEERS = 16
PIECES = 4
PER = ROWS // PIECES
WIDE = PER * C
PACK = PER * 8
EARLY = 1536
LATE = 512


def dot(left, right):
    return jnp.dot(left, right, preferred_element_type=F32)


def dot_nt(left, right):
    return lax.dot_general(left, right, (((1,), (1,)), ((), ())), preferred_element_type=F32)


def dot_tn(left, right):
    return lax.dot_general(left, right, (((0,), (0,)), ((), ())), preferred_element_type=F32)


def norm(values):
    average = jnp.sum(values, axis=0, keepdims=True) * (1.0 / C)
    centred = values - average
    inv_std = lax.rsqrt(jnp.sum(centred * centred, axis=0, keepdims=True) * (1.0 / C) + EPSILON)
    return centred * inv_std, inv_std


def norm_back(incoming, normed, inv_std, gain):
    scaled = incoming * gain
    first = jnp.sum(scaled, axis=0, keepdims=True) * (1.0 / C)
    second = jnp.sum(scaled * normed, axis=0, keepdims=True) * (1.0 / C)
    return inv_std * (scaled - first - normed * second)


def wide(block):
    return jnp.concatenate([block] * PER, axis=1) if PER > 1 else block


def split_rows(values):
    parts = [values[:, r * C:(r + 1) * C].reshape(PEERS, 8, C) for r in range(PER)]
    return jnp.concatenate(parts, axis=1) if PER > 1 else parts[0]


def join_rows(chunks):
    parts = [chunks[:, r * 8:(r + 1) * 8, :].reshape(C, C) for r in range(PER)]
    return jnp.concatenate(parts, axis=1) if PER > 1 else parts[0]


def kernel(
    ndp, scale,
    pair, cot, mask_s, mask_v, gains, w_proj, w_out, w_up, w_down,
    out_next, out_grad, out_proj, out_out, out_up, out_down, out_gains,
    gain_b, wpT, woT, wuT, wdT, wcat,
    pairT, lnT, hat0, rstd0, ag, av, bg, bv,
    s_l, r_l, s_r, r_r, s_t, r_t, s_d, r_d, s_dl, r_dl, s_dr, r_dr, s_n, r_c,
    x_l, x_r, lc, rc, y_l, y_r,
    tri_ln, hid, mid_ln, d_pre, d_mid, d_stack, d_val, cotT,
    g_e, rs_e, ch_e, ex_e, fin_e, ag_e, g_f, rs_f, ch_f, ex_f, fin_f, ag_f,
    send, recv, once, once_send, red, red_send,
):
    me = lax.axis_index("dap")
    my_dp = lax.axis_index("dp")
    barrier = pltpu.get_barrier_semaphore()

    def hello_dap(t, _):
        pl.semaphore_signal(barrier, inc=1, device_id={"dap": lax.rem(me + t, PEERS)}, device_id_type=MESH)
        return 0

    def hello_dp(t, _):
        pl.semaphore_signal(barrier, inc=1, device_id={"dp": lax.rem(my_dp + t, ndp)}, device_id_type=MESH)
        return 0

    lax.fori_loop(1, PEERS, hello_dap, 0)
    lax.fori_loop(1, ndp, hello_dp, 0)

    for n in range(3):
        gain_b[n] = jnp.broadcast_to(gains[n:n + 1, :], (C, C)).T
    for m in range(4):
        w_m = w_proj[m]
        wpT[m * C:(m + 1) * C, :] = w_m.astype(F32).T.astype(BF16)
        wcat[:, m * C:(m + 1) * C] = w_m
        f_at = slice(m * C, (m + 1) * C)
        wuT[f_at, :] = w_up[:, f_at].astype(F32).T.astype(BF16)
        wdT[:, f_at] = w_down[f_at, :].astype(F32).T.astype(BF16)
    for m in range(2):
        woT[m] = w_out[m].astype(F32).T.astype(BF16)
    wcat[:, 4 * C:5 * C] = w_out[0]
    g_e[1280:EARLY, :] = jnp.zeros((EARLY - 1280, C), BF16)

    pl.semaphore_wait(barrier, PEERS - 1 + ndp - 1)

    def exchange(which, src, dst, p):
        def body(t, _):
            d = lax.rem(me + t, PEERS)
            pltpu.make_async_remote_copy(
                src_ref=src.at[p, d], dst_ref=dst.at[p, me],
                send_sem=send.at[which], recv_sem=recv.at[which, p],
                device_id={"dap": d}, device_id_type=MESH,
            ).start()
            return 0

        lax.fori_loop(1, PEERS, body, 0)
        dst[p, me] = src[p, me]

    def arrived(which, dst, p):
        ref = dst.at[p, pl.ds(0, PEERS - 1)]
        pltpu.make_async_copy(ref, ref, recv.at[which, p]).wait()

    def sent(which, src):
        ref = src.at[:, pl.ds(0, PEERS - 1)]
        pltpu.make_async_copy(ref, ref, send.at[which]).wait()

    def cot_body(t, _):
        d = lax.rem(me + t, PEERS)
        pltpu.make_async_remote_copy(
            src_ref=cot.at[pl.ds(pl.multiple_of(d * 64, 64), 64)], dst_ref=r_c.at[me],
            send_sem=once_send.at[0], recv_sem=once.at[0],
            device_id={"dap": d}, device_id_type=MESH,
        ).start()
        return 0

    lax.fori_loop(1, PEERS, cot_body, 0)
    own_cot = pltpu.make_async_copy(cot.at[pl.ds(pl.multiple_of(me * 64, 64), 64)], r_c.at[me], once.at[1])
    own_cot.start()

    mask_k = mask_v[...].astype(F32)

    def mask_of(p):
        parts = []
        for r in range(PER):
            m_i = mask_s[0, me * ROWS + p * PER + r].astype(F32)
            parts.append(mask_k * m_i)
        return jnp.concatenate(parts, axis=1) if PER > 1 else parts[0]

    def columns(p):
        return pl.ds(pl.multiple_of(p * WIDE, WIDE), WIDE)

    def front(p, _):
        at = columns(p)
        x_rows = pair[at, :].astype(F32)
        x = jnp.concatenate([x_rows[r * C:(r + 1) * C, :].T for r in range(PER)], axis=1) if PER > 1 else x_rows.T
        pairT[:, at] = x
        normed, inv_std = norm(x)
        hat0[:, at] = normed
        rstd0[:, at] = inv_std
        ln = (normed * wide(gain_b[0])).astype(BF16)
        lnT[:, at] = ln
        mask = mask_of(p)
        gate = jax.nn.sigmoid(dot(wpT[0:C, :], ln))
        value = dot(wpT[C:2 * C, :], ln)
        ag[:, at] = gate
        av[:, at] = value
        s_l[p] = split_rows(mask * gate * value).astype(BF16)
        exchange(0, s_l, r_l, p)
        gate = jax.nn.sigmoid(dot(wpT[2 * C:3 * C, :], ln))
        value = dot(wpT[3 * C:4 * C, :], ln)
        bg[:, at] = gate
        bv[:, at] = value
        s_r[p] = split_rows(mask * gate * value).astype(BF16)
        exchange(1, s_r, r_r, p)
        return 0

    lax.fori_loop(0, PIECES, front, 0)

    def spread(dst, src, p):
        for s in range(PEERS):
            dst[pl.ds(pl.multiple_of(s * 64 + p * PACK, PACK), PACK), :] = src[p, s].astype(F32)

    def gather_chunks(p):
        return lambda ref: jnp.stack(
            [ref[pl.ds(pl.multiple_of(s * 64 + p * PACK, PACK), PACK), :] for s in range(PEERS)]
        ).astype(BF16)

    def take_l(p, _):
        arrived(0, r_l, p)
        spread(x_l, r_l, p)
        arrived(1, r_r, p)
        spread(x_r, r_r, p)
        return 0

    lax.fori_loop(0, PIECES, take_l, 0)

    def tri_body(c, _):
        left = x_l[pl.ds(c, C, 8), :].astype(BF16)
        right = x_r[pl.ds(c, C, 8), :].astype(BF16)
        lc[c] = left
        rc[c] = right
        y_l[pl.ds(c, C, 8), :] = dot_nt(left, right)
        return 0

    lax.fori_loop(0, 8, tri_body, 0)

    def tri_send(p, _):
        s_t[p] = gather_chunks(p)(y_l)
        exchange(2, s_t, r_t, p)
        return 0

    lax.fori_loop(0, PIECES, tri_send, 0)

    own_cot.wait()
    all_cot = r_c.at[pl.ds(0, PEERS - 1)]
    pltpu.make_async_copy(all_cot, all_cot, once.at[0]).wait()

    def next_body(p):
        rows = pl.ds(pl.multiple_of(me * 64 + p * PACK, PACK), PACK)

        def body(t, _):
            d = lax.rem(me + t, PEERS)
            pltpu.make_async_remote_copy(
                src_ref=s_n.at[p, d], dst_ref=out_next.at[rows],
                send_sem=once_send.at[1], recv_sem=once.at[2],
                device_id={"dap": d}, device_id_type=MESH,
            ).start()
            return 0

        lax.fori_loop(1, PEERS, body, 0)
        pltpu.make_async_copy(s_n.at[p, me], out_next.at[rows], once.at[3]).start()

    def middle(p, _):
        at = columns(p)
        arrived(2, r_t, p)
        tri = join_rows(r_t[p].astype(F32))
        tri_hat, tri_rstd = norm(tri)
        t_ln = (tri_hat * wide(gain_b[1])).astype(BF16)
        tri_ln[:, at] = t_ln
        out_gate = jax.nn.sigmoid(dot(woT[0], lnT[:, at]))
        out_value = dot(woT[1], t_ln)
        mid = (pairT[:, at] + out_gate * out_value).astype(BF16).astype(F32)
        mid_hat, mid_rstd = norm(mid)
        m_ln = (mid_hat * wide(gain_b[2])).astype(BF16)
        mid_ln[:, at] = m_ln
        cot_rows = r_c[:, pl.ds(pl.multiple_of(p * PACK, PACK), PACK), :].astype(F32)
        cot_t = jnp.concatenate(
            [cot_rows[:, r * 8:(r + 1) * 8, :].reshape(C, C).T for r in range(PER)], axis=1
        )
        cot_b = cot_t.astype(BF16)
        cotT[:, at] = cot_b
        for f in range(4):
            f_at = slice(f * C, (f + 1) * C)
            u = dot(wuT[f_at, :], m_ln)
            square = u * u
            tanh = jnp.tanh(u * (GELU_SCALE + GELU_SCALE * GELU_CUBIC * square))
            half = 0.5 + 0.5 * tanh
            act = u * half
            slope = half + act * (1.0 - tanh) * (GELU_SCALE + 3.0 * GELU_SCALE * GELU_CUBIC * square)
            hid[f_at, at] = act.astype(BF16)
            d_pre[f_at, at] = (dot(w_down[f_at, :], cot_b) * slope).astype(BF16)
        d_mid_v = cot_t + norm_back(dot(w_up[...], d_pre[:, at]), mid_hat, mid_rstd, wide(gain_b[2]))
        d_mid[:, at] = d_mid_v
        d_gate = (d_mid_v * out_value * out_gate * (1.0 - out_gate)).astype(BF16)
        d_stack[4 * C:5 * C, at] = d_gate
        d_value = (d_mid_v * out_gate).astype(BF16)
        d_val[:, at] = d_value
        d_tri = norm_back(dot(w_out[1], d_value), tri_hat, tri_rstd, wide(gain_b[1]))
        s_d[p] = split_rows(d_tri).astype(BF16)
        exchange(3, s_d, r_d, p)
        nxt = mid + dot(wdT[...], hid[:, at])
        nxt_rows = jnp.concatenate(
            [nxt[:, r * C:(r + 1) * C].T.reshape(PEERS, 8, C) for r in range(PER)], axis=1
        )
        s_n[p] = nxt_rows.astype(BF16)
        next_body(p)
        return 0

    lax.fori_loop(0, PIECES, middle, 0)

    def reduce_scatter(which, src, dst, rows):
        def body(t, _):
            q = lax.rem(my_dp + t, ndp)
            pltpu.make_async_remote_copy(
                src_ref=src.at[pl.ds(pl.multiple_of(q * rows, 16), rows)], dst_ref=dst.at[my_dp],
                send_sem=red_send.at[which], recv_sem=red.at[which],
                device_id={"dp": q}, device_id_type=MESH,
            ).start()
            return 0

        lax.fori_loop(1, ndp, body, 0)
        dst[my_dp] = src[pl.ds(pl.multiple_of(my_dp * rows, 16), rows), :]

    def wait_count(ref, sem):
        pltpu.make_async_copy(ref, ref, sem).wait()

    def total(ref, count):
        def body(n, value):
            return value + ref[n].astype(F32)

        return lax.fori_loop(1, count, body, ref[0].astype(F32))

    def cross(which, src, dst):
        def body(t, _):
            d = lax.rem(me + t, PEERS)
            pltpu.make_async_remote_copy(
                src_ref=src, dst_ref=dst.at[me],
                send_sem=red_send.at[which], recv_sem=red.at[which],
                device_id={"dap": d}, device_id_type=MESH,
            ).start()
            return 0

        lax.fori_loop(1, PEERS, body, 0)
        dst[me] = src[...]

    def all_gather(which, src, dst, rows):
        place = pl.ds(pl.multiple_of(my_dp * rows, 16), rows)

        def body(t, _):
            q = lax.rem(my_dp + t, ndp)
            pltpu.make_async_remote_copy(
                src_ref=src, dst_ref=dst.at[place],
                send_sem=red_send.at[which], recv_sem=red.at[which],
                device_id={"dp": q}, device_id_type=MESH,
            ).start()
            return 0

        lax.fori_loop(1, ndp, body, 0)
        dst[place, :] = src[...]

    rows_e, rows_f = EARLY // ndp, LATE // ndp

    for f in range(4):
        f_at = slice(f * C, (f + 1) * C)
        g_e[f_at, :] = dot_nt(mid_ln[...], d_pre[f_at, :]).astype(BF16)
        g_e[512 + f * C:512 + (f + 1) * C, :] = dot_nt(hid[f_at, :], cotT[...]).astype(BF16)
    g_e[1024:1152, :] = dot_nt(lnT[...], d_stack[4 * C:5 * C, :]).astype(BF16)
    g_e[1152:1280, :] = dot_nt(tri_ln[...], d_val[...]).astype(BF16)
    reduce_scatter(0, g_e, rs_e, rows_e)

    def take_d(p, _):
        arrived(3, r_d, p)
        spread(x_l, r_d, p)
        return 0

    lax.fori_loop(0, PIECES, take_d, 0)

    def back_body(c, _):
        grad = x_l[pl.ds(c, C, 8), :].astype(BF16)
        y_l[pl.ds(c, C, 8), :] = dot(grad, rc[c])
        y_r[pl.ds(c, C, 8), :] = dot_tn(grad, lc[c])
        return 0

    lax.fori_loop(0, 8, back_body, 0)

    def back_send(p, _):
        s_dl[p] = gather_chunks(p)(y_l)
        exchange(4, s_dl, r_dl, p)
        s_dr[p] = gather_chunks(p)(y_r)
        exchange(5, s_dr, r_dr, p)
        return 0

    lax.fori_loop(0, PIECES, back_send, 0)

    wait_count(rs_e.at[pl.ds(0, ndp - 1)], red.at[0])
    ch_e[...] = total(rs_e, ndp).astype(BF16)
    cross(1, ch_e, ex_e)

    def lower(p, _):
        at = columns(p)
        mask = mask_of(p)
        arrived(4, r_dl, p)
        grad = join_rows(r_dl[p].astype(F32)) * mask
        gate = ag[:, at]
        with_gate = grad * gate
        d_stack[0:C, at] = (with_gate * av[:, at] * (1.0 - gate)).astype(BF16)
        d_stack[C:2 * C, at] = with_gate.astype(BF16)
        arrived(5, r_dr, p)
        grad = join_rows(r_dr[p].astype(F32)) * mask
        gate = bg[:, at]
        with_gate = grad * gate
        d_stack[2 * C:3 * C, at] = (with_gate * bv[:, at] * (1.0 - gate)).astype(BF16)
        d_stack[3 * C:4 * C, at] = with_gate.astype(BF16)
        d_ln = dot(wcat[...], d_stack[:, at])
        result = d_mid[:, at] + norm_back(d_ln, hat0[:, at], rstd0[:, at], wide(gain_b[0]))
        for r in range(PER):
            row = pl.ds(pl.multiple_of(p * WIDE + r * C, C), C)
            out_grad[row, :] = result[:, r * C:(r + 1) * C].T.astype(BF16)
        return 0

    lax.fori_loop(0, PIECES, lower, 0)

    for m in range(4):
        m_at = slice(m * C, (m + 1) * C)
        g_f[m_at, :] = dot_nt(lnT[...], d_stack[m_at, :]).astype(BF16)
    reduce_scatter(2, g_f, rs_f, rows_f)

    wait_count(ex_e.at[pl.ds(0, PEERS - 1)], red.at[1])
    fin_e[...] = (total(ex_e, PEERS) * scale).astype(BF16)
    all_gather(4, fin_e, ag_e, rows_e)

    wait_count(rs_f.at[pl.ds(0, ndp - 1)], red.at[2])
    ch_f[...] = total(rs_f, ndp).astype(BF16)
    cross(3, ch_f, ex_f)
    wait_count(ex_f.at[pl.ds(0, PEERS - 1)], red.at[3])
    fin_f[...] = (total(ex_f, PEERS) * scale).astype(BF16)
    all_gather(5, fin_f, ag_f, rows_f)

    wait_count(ag_e.at[pl.ds(0, (ndp - 1) * rows_e)], red.at[4])
    mid_sum = jnp.zeros((C, C), F32)
    for f in range(4):
        f_at = slice(f * C, (f + 1) * C)
        block = ag_e[f_at, :]
        out_up[:, f_at] = block
        mid_sum = mid_sum + block.astype(F32) * w_up[:, f_at].astype(F32)
    out_down[...] = ag_e[512:1024, :]
    out_out[...] = ag_e[1024:1280, :]
    pair_sum = ag_e[1024:1152, :].astype(F32) * w_out[0].astype(F32)
    tri_sum = ag_e[1152:1280, :].astype(F32) * w_out[1].astype(F32)

    wait_count(ag_f.at[pl.ds(0, (ndp - 1) * rows_f)], red.at[5])
    for m in range(4):
        block = ag_f[m * C:(m + 1) * C, :]
        pair_sum = pair_sum + block.astype(F32) * w_proj[m].astype(F32)
    out_proj[...] = ag_f[...]
    sums = [jnp.sum(s.T, axis=0, keepdims=True) for s in (pair_sum, tri_sum, mid_sum)]
    out_gains[...] = (jnp.concatenate(sums, axis=0) / gains[...]).astype(BF16)

    for which, src in enumerate((s_l, s_r, s_t, s_d, s_dl, s_dr)):
        sent(which, src)
    sent_cot = r_c.at[pl.ds(0, PEERS - 1)]
    wait_count(sent_cot, once_send.at[0])
    all_next = s_n.at[:, pl.ds(0, PEERS - 1)]
    wait_count(all_next, once_send.at[1])
    wait_count(all_next, once.at[2])
    wait_count(s_n.at[:, 0], once.at[3])
    wait_count(rs_e.at[pl.ds(0, ndp - 1)], red_send.at[0])
    wait_count(ex_e.at[pl.ds(0, PEERS - 1)], red_send.at[1])
    wait_count(rs_f.at[pl.ds(0, ndp - 1)], red_send.at[2])
    wait_count(ex_f.at[pl.ds(0, PEERS - 1)], red_send.at[3])
    wait_count(ag_e.at[pl.ds(0, (ndp - 1) * rows_e)], red_send.at[4])
    wait_count(ag_f.at[pl.ds(0, (ndp - 1) * rows_f)], red_send.at[5])


def local(ndp, pair_repr, cotangent, residue_mask, norm_gains, w_proj, w_out, w_up, w_down):
    scale = 1.0 / math.sqrt(ndp * C * C)
    vmem = pl.BlockSpec(memory_space=pltpu.VMEM)
    smem = pl.BlockSpec(memory_space=pltpu.SMEM)
    hbm = pl.BlockSpec(memory_space=pl.ANY)
    columns = ROWS * C
    chunks = pltpu.VMEM((PIECES, PEERS, PACK, C), BF16)
    full = pltpu.VMEM((C, columns), F32)
    half = pltpu.VMEM((C, columns), BF16)
    big = pltpu.VMEM((FFN, columns), BF16)
    cube = pltpu.VMEM((1024, C), F32)
    rows_e, rows_f = EARLY // ndp, LATE // ndp
    scratch = [
        pltpu.VMEM((3, C, C), F32),
        pltpu.VMEM((4 * C, C), BF16),
        pltpu.VMEM((2, C, C), BF16),
        pltpu.VMEM((FFN, C), BF16),
        pltpu.VMEM((C, FFN), BF16),
        pltpu.VMEM((C, 5 * C), BF16),
        full, half, full, pltpu.VMEM((1, columns), F32), full, full, full, full,
        *([chunks] * 13),
        pltpu.VMEM((PEERS, 64, C), BF16),
        cube, cube, pltpu.VMEM((8, C, C), BF16), pltpu.VMEM((8, C, C), BF16), cube, cube,
        half, big, half, big, full, pltpu.VMEM((5 * C, columns), BF16), half, half,
    ]
    for rows, whole in ((rows_e, EARLY), (rows_f, LATE)):
        scratch += [
            pltpu.VMEM((whole, C), BF16),
            pltpu.VMEM((ndp, rows, C), BF16),
            pltpu.VMEM((rows, C), BF16),
            pltpu.VMEM((PEERS, rows, C), BF16),
            pltpu.VMEM((rows, C), BF16),
            pltpu.VMEM((whole, C), BF16),
        ]
    scratch += [
        pltpu.SemaphoreType.DMA((6,)),
        pltpu.SemaphoreType.DMA((6, PIECES)),
        pltpu.SemaphoreType.DMA((4,)),
        pltpu.SemaphoreType.DMA((2,)),
        pltpu.SemaphoreType.DMA((6,)),
        pltpu.SemaphoreType.DMA((6,)),
    ]
    results = pl.pallas_call(
        functools.partial(kernel, ndp, scale),
        out_shape=(
            jax.ShapeDtypeStruct((1024, C), BF16),
            jax.ShapeDtypeStruct((1024, C), BF16),
            jax.ShapeDtypeStruct((4 * C, C), BF16),
            jax.ShapeDtypeStruct((2 * C, C), BF16),
            jax.ShapeDtypeStruct((C, FFN), BF16),
            jax.ShapeDtypeStruct((FFN, C), BF16),
            jax.ShapeDtypeStruct((3, C), BF16),
        ),
        in_specs=[vmem, hbm, smem, vmem, vmem, vmem, vmem, vmem, vmem],
        out_specs=(hbm, vmem, vmem, vmem, vmem, vmem, vmem),
        scratch_shapes=scratch,
        compiler_params=pltpu.CompilerParams(
            collective_id=0, has_side_effects=True, vmem_limit_bytes=48 * 1024 * 1024
        ),
        cost_estimate=pl.CostEstimate(flops=1_600_000_000, bytes_accessed=3_000_000, transcendentals=1_200_000),
    )(
        pair_repr.reshape(1024, C), cotangent.reshape(1024, C), residue_mask, residue_mask,
        norm_gains, w_proj, w_out, w_up, w_down,
    )
    nxt, grad, g_proj, g_out, g_up, g_down, g_gains = results
    return (
        nxt.reshape(1, C, ROWS, C),
        grad.reshape(1, ROWS, C, C),
        g_proj.reshape(4, C, C),
        g_out.reshape(2, C, C),
        g_up,
        g_down,
        g_gains,
    )


def solution(mesh):
    in_specs = (
        P("dp", "dap", None, None),
        P("dp", None, "dap", None),
        P("dp", None),
        P(),
        P(),
        P(),
        P(),
        P(),
    )
    out_specs = (P("dp", None, "dap", None), P("dp", "dap", None, None), P(), P(), P(), P(), P())
    body = functools.partial(local, mesh.shape["dp"])
    return jax.shard_map(body, mesh=mesh, in_specs=in_specs, out_specs=out_specs, check_vma=False)
```

```python
import functools
import math

import jax
import jax.numpy as jnp
from jax import lax
from jax.experimental import pallas as pl
from jax.experimental.pallas import tpu as pltpu
from jax.sharding import PartitionSpec as P

EPSILON = 1e-05
GELU_SCALE = 0.7978845608028654
GELU_CUBIC = 0.044715
MESH = pl.DeviceIdType.MESH
F32 = jnp.float32
BF16 = jnp.bfloat16

C = 128
FFN = 512
ROWS = 8
PEERS = 16
PIECES = 4
PER = ROWS // PIECES
WIDE = PER * C
PACK = PER * 8
EARLY = 1536
LATE = 512


AWAY = sorted(
    [(dy, dx) for dy in range(-3, 5) for dx in range(2) if dy or dx],
    key=lambda at: (-abs(at[0]) - 2 * at[1], at[0]),
)


def far_crops(ndp):
    depth = max(1, ndp // 4)
    steps = [(dz, dr) for dz in range(-((depth - 1) // 2), depth // 2 + 1) for dr in range(ndp // depth) if dz or dr]
    return sorted(steps, key=lambda at: (-abs(at[0]) - at[1] // 2, -at[1], at[0]))


def dot(left, right):
    return jnp.dot(left, right, preferred_element_type=F32)


def dot_nt(left, right):
    return lax.dot_general(left, right, (((1,), (1,)), ((), ())), preferred_element_type=F32)


def dot_tn(left, right):
    return lax.dot_general(left, right, (((0,), (0,)), ((), ())), preferred_element_type=F32)


def norm(values):
    average = jnp.sum(values, axis=0, keepdims=True) * (1.0 / C)
    centred = values - average
    inv_std = lax.rsqrt(jnp.sum(centred * centred, axis=0, keepdims=True) * (1.0 / C) + EPSILON)
    return centred * inv_std, inv_std


def norm_back(incoming, normed, inv_std, gain):
    scaled = incoming * gain
    first = jnp.sum(scaled, axis=0, keepdims=True) * (1.0 / C)
    second = jnp.sum(scaled * normed, axis=0, keepdims=True) * (1.0 / C)
    return inv_std * (scaled - first - normed * second)


def wide(block):
    return jnp.concatenate([block] * PER, axis=1) if PER > 1 else block


def split_rows(values):
    parts = [values[:, r * C:(r + 1) * C].reshape(PEERS, 8, C) for r in range(PER)]
    return jnp.concatenate(parts, axis=1) if PER > 1 else parts[0]


def join_rows(chunks):
    parts = [chunks[:, r * 8:(r + 1) * 8, :].reshape(C, C) for r in range(PER)]
    return jnp.concatenate(parts, axis=1) if PER > 1 else parts[0]


def kernel(
    ndp, scale,
    pair_h, cot, mask_h, gains_h, w_proj_h, w_out_h, w_up_h, w_down_h,
    out_next, out_grad_h, out_proj_h, out_out_h, out_up_h, out_down_h, out_gains_h,
    pair, mask_v, gains, w_proj, w_out, w_up, w_down,
    out_grad, out_proj, out_out, out_up, out_down, out_gains, in_sem, out_sem,
    mask_b, gain_b, wpT, woT, wuT, wdT, wcat,
    pairT, lnT, hat0, rstd0, ag, av, bg, bv,
    s_l, r_l, s_r, r_r, s_t, r_t, s_d, r_d, s_dl, r_dl, s_dr, r_dr, s_n, r_c,
    x_l, x_r, lc, rc, y_l, y_r,
    tri_ln, hid, mid_ln, d_pre, d_mid, d_stack, d_val, cotT,
    g_e, rs_e, ch_e, ex_e, fin_e, ag_e, g_f, rs_f, ch_f, ex_f, fin_f, ag_f,
    send, recv, once, once_send, red, red_send,
):
    me = lax.axis_index("dap")
    my_dp = lax.axis_index("dp")
    barrier = pltpu.get_barrier_semaphore()

    def peer(dy, dx):
        return lax.rem(me // 2 + dy + 8, 8) * 2 + lax.rem(me + dx, 2)

    depth = max(1, ndp // 4)
    near = ndp // depth
    crops = far_crops(ndp)

    def crop(dz, dr):
        here = lax.rem(my_dp, near)
        if near == 4:
            there = lax.rem(here // 2 + dr // 2, 2) * 2 + lax.rem(here + dr, 2)
        else:
            there = lax.rem(here + dr, near)
        return lax.rem(my_dp // near + dz + depth, depth) * near + there

    for dy, dx in AWAY:
        pl.semaphore_signal(barrier, inc=1, device_id={"dap": peer(dy, dx)}, device_id_type=MESH)
    for dz, dr in crops:
        pl.semaphore_signal(barrier, inc=1, device_id={"dp": crop(dz, dr)}, device_id_type=MESH)

    loads = [
        pltpu.make_async_copy(src, dst, in_sem.at[n])
        for n, (src, dst) in enumerate((
            (pair_h, pair), (mask_h, mask_v), (gains_h, gains), (w_proj_h, w_proj),
            (w_out_h, w_out), (w_up_h, w_up), (w_down_h, w_down),
        ))
    ]
    for load in loads:
        load.start()
    for load in loads[1:4]:
        load.wait()

    mask_k = mask_v[...].astype(F32)
    mask_b[...] = jnp.broadcast_to(mask_k, (C, C)).T
    for n in range(3):
        gain_b[n] = jnp.broadcast_to(gains[n:n + 1, :], (C, C)).T
    for m in range(4):
        w_m = w_proj[m]
        wpT[m * C:(m + 1) * C, :] = w_m.astype(F32).T.astype(BF16)
        wcat[:, m * C:(m + 1) * C] = w_m
    loads[0].wait()

    def exchange(which, src, dst, p):
        for dy, dx in AWAY:
            d = peer(dy, dx)
            pltpu.make_async_remote_copy(
                src_ref=src.at[p, d], dst_ref=dst.at[p, me],
                send_sem=send.at[which], recv_sem=recv.at[which, p],
                device_id={"dap": d}, device_id_type=MESH,
            ).start()
        dst[p, me] = src[p, me]

    def arrived(which, dst, p):
        ref = dst.at[p, pl.ds(0, PEERS - 1)]
        pltpu.make_async_copy(ref, ref, recv.at[which, p]).wait()

    def sent(which, src):
        ref = src.at[:, pl.ds(0, PEERS - 1)]
        pltpu.make_async_copy(ref, ref, send.at[which]).wait()

    def mask_of(p):
        parts = []
        for r in range(PER):
            parts.append(mask_k * mask_b[pl.ds(me * ROWS + p * PER + r, 1), :])
        return jnp.concatenate(parts, axis=1) if PER > 1 else parts[0]

    def columns(p):
        return pl.ds(pl.multiple_of(p * WIDE, WIDE), WIDE)

    def front(p):
        at = columns(p)
        x_rows = pair[at, :].astype(F32)
        x = jnp.concatenate([x_rows[r * C:(r + 1) * C, :].T for r in range(PER)], axis=1) if PER > 1 else x_rows.T
        pairT[:, at] = x
        normed, inv_std = norm(x)
        hat0[:, at] = normed
        rstd0[:, at] = inv_std
        ln = (normed * wide(gain_b[0])).astype(BF16)
        lnT[:, at] = ln
        mask = mask_of(p)
        gate = jax.nn.sigmoid(dot(wpT[0:C, :], ln))
        value = dot(wpT[C:2 * C, :], ln)
        ag[:, at] = gate
        av[:, at] = value
        s_l[p] = split_rows(mask * gate * value).astype(BF16)
        gate = jax.nn.sigmoid(dot(wpT[2 * C:3 * C, :], ln))
        value = dot(wpT[3 * C:4 * C, :], ln)
        bg[:, at] = gate
        bv[:, at] = value
        s_r[p] = split_rows(mask * gate * value).astype(BF16)

    def front_send(p):
        exchange(0, s_l, r_l, p)
        exchange(1, s_r, r_r, p)

    def front_step(p, _):
        front_send(p)
        front(p + 1)
        return 0

    front(0)
    pl.semaphore_wait(barrier, PEERS - 1 + ndp - 1)
    lax.fori_loop(0, PIECES - 1, front_step, 0)
    front_send(PIECES - 1)

    for dy, dx in AWAY:
        d = peer(dy, dx)
        pltpu.make_async_remote_copy(
            src_ref=cot.at[pl.ds(pl.multiple_of(d * 64, 64), 64)], dst_ref=r_c.at[me],
            send_sem=once_send.at[0], recv_sem=once.at[0],
            device_id={"dap": d}, device_id_type=MESH,
        ).start()
    own_cot = pltpu.make_async_copy(cot.at[pl.ds(pl.multiple_of(me * 64, 64), 64)], r_c.at[me], once.at[1])
    own_cot.start()

    for load in loads[4:]:
        load.wait()
    for m in range(4):
        f_at = slice(m * C, (m + 1) * C)
        wuT[f_at, :] = w_up[:, f_at].astype(F32).T.astype(BF16)
        wdT[:, f_at] = w_down[f_at, :].astype(F32).T.astype(BF16)
    for m in range(2):
        woT[m] = w_out[m].astype(F32).T.astype(BF16)
    wcat[:, 4 * C:5 * C] = w_out[0]
    g_e[1280:EARLY, :] = jnp.zeros((EARLY - 1280, C), BF16)

    def spread(dst, src, p):
        for s in range(PEERS):
            dst[pl.ds(pl.multiple_of(s * 64 + p * PACK, PACK), PACK), :] = src[p, s].astype(F32)

    def gather_chunks(p):
        return lambda ref: jnp.stack(
            [ref[pl.ds(pl.multiple_of(s * 64 + p * PACK, PACK), PACK), :] for s in range(PEERS)]
        ).astype(BF16)

    def take_l(p, _):
        arrived(0, r_l, p)
        spread(x_l, r_l, p)
        arrived(1, r_r, p)
        spread(x_r, r_r, p)
        return 0

    lax.fori_loop(0, PIECES, take_l, 0)

    def tri_body(c, _):
        left = x_l[pl.ds(c, C, 8), :].astype(BF16)
        right = x_r[pl.ds(c, C, 8), :].astype(BF16)
        lc[c] = left
        rc[c] = right
        y_l[pl.ds(c, C, 8), :] = dot_nt(left, right)
        return 0

    lax.fori_loop(0, 8, tri_body, 0)

    def tri_send(p, _):
        s_t[p] = gather_chunks(p)(y_l)
        exchange(2, s_t, r_t, p)
        return 0

    lax.fori_loop(0, PIECES, tri_send, 0)

    own_cot.wait()
    all_cot = r_c.at[pl.ds(0, PEERS - 1)]
    pltpu.make_async_copy(all_cot, all_cot, once.at[0]).wait()

    def next_body(p):
        rows = pl.ds(pl.multiple_of(me * 64 + p * PACK, PACK), PACK)

        for dy, dx in AWAY:
            d = peer(dy, dx)
            pltpu.make_async_remote_copy(
                src_ref=s_n.at[p, d], dst_ref=out_next.at[rows],
                send_sem=once_send.at[1], recv_sem=once.at[2],
                device_id={"dap": d}, device_id_type=MESH,
            ).start()
        pltpu.make_async_copy(s_n.at[p, me], out_next.at[rows], once.at[3]).start()

    def middle(p, _):
        at = columns(p)
        arrived(2, r_t, p)
        tri = join_rows(r_t[p].astype(F32))
        tri_hat, tri_rstd = norm(tri)
        t_ln = (tri_hat * wide(gain_b[1])).astype(BF16)
        tri_ln[:, at] = t_ln
        out_gate = jax.nn.sigmoid(dot(woT[0], lnT[:, at]))
        out_value = dot(woT[1], t_ln)
        mid = (pairT[:, at] + out_gate * out_value).astype(BF16).astype(F32)
        mid_hat, mid_rstd = norm(mid)
        m_ln = (mid_hat * wide(gain_b[2])).astype(BF16)
        mid_ln[:, at] = m_ln
        cot_rows = r_c[:, pl.ds(pl.multiple_of(p * PACK, PACK), PACK), :].astype(F32)
        cot_t = jnp.concatenate(
            [cot_rows[:, r * 8:(r + 1) * 8, :].reshape(C, C).T for r in range(PER)], axis=1
        )
        cot_b = cot_t.astype(BF16)
        cotT[:, at] = cot_b
        for f in range(4):
            f_at = slice(f * C, (f + 1) * C)
            u = dot(wuT[f_at, :], m_ln)
            square = u * u
            tanh = jnp.tanh(u * (GELU_SCALE + GELU_SCALE * GELU_CUBIC * square))
            half = 0.5 + 0.5 * tanh
            act = u * half
            slope = half + act * (1.0 - tanh) * (GELU_SCALE + 3.0 * GELU_SCALE * GELU_CUBIC * square)
            hid[f_at, at] = act.astype(BF16)
            d_pre[f_at, at] = (dot(w_down[f_at, :], cot_b) * slope).astype(BF16)
        d_mid_v = cot_t + norm_back(dot(w_up[...], d_pre[:, at]), mid_hat, mid_rstd, wide(gain_b[2]))
        d_mid[:, at] = d_mid_v
        d_gate = (d_mid_v * out_value * out_gate * (1.0 - out_gate)).astype(BF16)
        d_stack[4 * C:5 * C, at] = d_gate
        d_value = (d_mid_v * out_gate).astype(BF16)
        d_val[:, at] = d_value
        d_tri = norm_back(dot(w_out[1], d_value), tri_hat, tri_rstd, wide(gain_b[1]))
        s_d[p] = split_rows(d_tri).astype(BF16)
        exchange(3, s_d, r_d, p)
        nxt = mid + dot(wdT[...], hid[:, at])
        nxt_rows = jnp.concatenate(
            [nxt[:, r * C:(r + 1) * C].T.reshape(PEERS, 8, C) for r in range(PER)], axis=1
        )
        s_n[p] = nxt_rows.astype(BF16)
        return 0

    lax.fori_loop(0, PIECES, middle, 0)

    def send_next(p, _):
        next_body(p)
        return 0

    lax.fori_loop(0, PIECES, send_next, 0)

    def reduce_scatter(which, src, dst, rows):
        for dz, dr in crops:
            q = crop(dz, dr)
            pltpu.make_async_remote_copy(
                src_ref=src.at[pl.ds(pl.multiple_of(q * rows, 16), rows)], dst_ref=dst.at[my_dp],
                send_sem=red_send.at[which], recv_sem=red.at[which],
                device_id={"dp": q}, device_id_type=MESH,
            ).start()
        dst[my_dp] = src[pl.ds(pl.multiple_of(my_dp * rows, 16), rows), :]

    def wait_count(ref, sem):
        pltpu.make_async_copy(ref, ref, sem).wait()

    def total(ref, count):
        def body(n, value):
            return value + ref[n].astype(F32)

        return lax.fori_loop(1, count, body, ref[0].astype(F32))

    def cross(which, src, dst):
        for dy, dx in AWAY:
            pltpu.make_async_remote_copy(
                src_ref=src, dst_ref=dst.at[me],
                send_sem=red_send.at[which], recv_sem=red.at[which],
                device_id={"dap": peer(dy, dx)}, device_id_type=MESH,
            ).start()
        dst[me] = src[...]

    def all_gather(which, src, dst, rows):
        place = pl.ds(pl.multiple_of(my_dp * rows, 16), rows)

        for dz, dr in crops:
            pltpu.make_async_remote_copy(
                src_ref=src, dst_ref=dst.at[place],
                send_sem=red_send.at[which], recv_sem=red.at[which],
                device_id={"dp": crop(dz, dr)}, device_id_type=MESH,
            ).start()
        dst[place, :] = src[...]

    rows_e, rows_f = EARLY // ndp, LATE // ndp

    for f in range(4):
        f_at = slice(f * C, (f + 1) * C)
        g_e[f_at, :] = dot_nt(mid_ln[...], d_pre[f_at, :]).astype(BF16)
        g_e[512 + f * C:512 + (f + 1) * C, :] = dot_nt(hid[f_at, :], cotT[...]).astype(BF16)
    g_e[1024:1152, :] = dot_nt(lnT[...], d_stack[4 * C:5 * C, :]).astype(BF16)
    g_e[1152:1280, :] = dot_nt(tri_ln[...], d_val[...]).astype(BF16)
    reduce_scatter(0, g_e, rs_e, rows_e)

    def take_d(p, _):
        arrived(3, r_d, p)
        spread(x_l, r_d, p)
        return 0

    lax.fori_loop(0, PIECES, take_d, 0)

    def back_body(c, _):
        grad = x_l[pl.ds(c, C, 8), :].astype(BF16)
        y_l[pl.ds(c, C, 8), :] = dot(grad, rc[c])
        y_r[pl.ds(c, C, 8), :] = dot_tn(grad, lc[c])
        return 0

    lax.fori_loop(0, 8, back_body, 0)

    def back_send(p, _):
        s_dl[p] = gather_chunks(p)(y_l)
        exchange(4, s_dl, r_dl, p)
        s_dr[p] = gather_chunks(p)(y_r)
        exchange(5, s_dr, r_dr, p)
        return 0

    lax.fori_loop(0, PIECES, back_send, 0)

    wait_count(rs_e.at[pl.ds(0, ndp - 1)], red.at[0])
    ch_e[...] = total(rs_e, ndp).astype(BF16)
    cross(1, ch_e, ex_e)

    def lower(p, _):
        at = columns(p)
        mask = mask_of(p)
        arrived(4, r_dl, p)
        grad = join_rows(r_dl[p].astype(F32)) * mask
        gate = ag[:, at]
        with_gate = grad * gate
        d_stack[0:C, at] = (with_gate * av[:, at] * (1.0 - gate)).astype(BF16)
        d_stack[C:2 * C, at] = with_gate.astype(BF16)
        arrived(5, r_dr, p)
        grad = join_rows(r_dr[p].astype(F32)) * mask
        gate = bg[:, at]
        with_gate = grad * gate
        d_stack[2 * C:3 * C, at] = (with_gate * bv[:, at] * (1.0 - gate)).astype(BF16)
        d_stack[3 * C:4 * C, at] = with_gate.astype(BF16)
        d_ln = dot(wcat[...], d_stack[:, at])
        result = d_mid[:, at] + norm_back(d_ln, hat0[:, at], rstd0[:, at], wide(gain_b[0]))
        for r in range(PER):
            row = pl.ds(pl.multiple_of(p * WIDE + r * C, C), C)
            out_grad[row, :] = result[:, r * C:(r + 1) * C].T.astype(BF16)
        return 0

    lax.fori_loop(0, PIECES, lower, 0)

    def put(n, src, dst):
        copy = pltpu.make_async_copy(src, dst, out_sem.at[n])
        copy.start()
        return copy

    puts = [put(0, out_grad, out_grad_h)]

    for m in range(4):
        m_at = slice(m * C, (m + 1) * C)
        g_f[m_at, :] = dot_nt(lnT[...], d_stack[m_at, :]).astype(BF16)
    reduce_scatter(2, g_f, rs_f, rows_f)

    wait_count(ex_e.at[pl.ds(0, PEERS - 1)], red.at[1])
    fin_e[...] = (total(ex_e, PEERS) * scale).astype(BF16)
    all_gather(4, fin_e, ag_e, rows_e)

    wait_count(rs_f.at[pl.ds(0, ndp - 1)], red.at[2])
    ch_f[...] = total(rs_f, ndp).astype(BF16)
    cross(3, ch_f, ex_f)
    wait_count(ex_f.at[pl.ds(0, PEERS - 1)], red.at[3])
    fin_f[...] = (total(ex_f, PEERS) * scale).astype(BF16)
    all_gather(5, fin_f, ag_f, rows_f)

    wait_count(ag_e.at[pl.ds(0, (ndp - 1) * rows_e)], red.at[4])
    mid_sum = jnp.zeros((C, C), F32)
    for f in range(4):
        f_at = slice(f * C, (f + 1) * C)
        block = ag_e[f_at, :]
        out_up[:, f_at] = block
        mid_sum = mid_sum + block.astype(F32) * w_up[:, f_at].astype(F32)
    out_down[...] = ag_e[512:1024, :]
    out_out[...] = ag_e[1024:1280, :]
    puts += [put(1, out_up, out_up_h), put(2, out_down, out_down_h), put(3, out_out, out_out_h)]
    pair_sum = ag_e[1024:1152, :].astype(F32) * w_out[0].astype(F32)
    tri_sum = ag_e[1152:1280, :].astype(F32) * w_out[1].astype(F32)

    wait_count(ag_f.at[pl.ds(0, (ndp - 1) * rows_f)], red.at[5])
    for m in range(4):
        block = ag_f[m * C:(m + 1) * C, :]
        pair_sum = pair_sum + block.astype(F32) * w_proj[m].astype(F32)
    out_proj[...] = ag_f[...]
    sums = [jnp.sum(s.T, axis=0, keepdims=True) for s in (pair_sum, tri_sum, mid_sum)]
    out_gains[...] = (jnp.concatenate(sums, axis=0) / gains[...]).astype(BF16)
    puts += [put(4, out_proj, out_proj_h), put(5, out_gains, out_gains_h)]

    for copy in puts:
        copy.wait()
    for which, src in enumerate((s_l, s_r, s_t, s_d, s_dl, s_dr)):
        sent(which, src)
    sent_cot = r_c.at[pl.ds(0, PEERS - 1)]
    wait_count(sent_cot, once_send.at[0])
    all_next = s_n.at[:, pl.ds(0, PEERS - 1)]
    wait_count(all_next, once_send.at[1])
    wait_count(all_next, once.at[2])
    wait_count(s_n.at[:, 0], once.at[3])
    wait_count(rs_e.at[pl.ds(0, ndp - 1)], red_send.at[0])
    wait_count(ex_e.at[pl.ds(0, PEERS - 1)], red_send.at[1])
    wait_count(rs_f.at[pl.ds(0, ndp - 1)], red_send.at[2])
    wait_count(ex_f.at[pl.ds(0, PEERS - 1)], red_send.at[3])
    wait_count(ag_e.at[pl.ds(0, (ndp - 1) * rows_e)], red_send.at[4])
    wait_count(ag_f.at[pl.ds(0, (ndp - 1) * rows_f)], red_send.at[5])


def hand_over(outs, results):
    count = len(outs)

    def copies(*refs):
        held = refs[2 * count:3 * count]
        sems = refs[3 * count]
        takes = [pltpu.make_async_copy(refs[n], held[n], sems.at[0, n]) for n in range(count)]
        gives = [pltpu.make_async_copy(held[n], refs[count + n], sems.at[1, n]) for n in range(count)]
        for take in takes:
            take.start()
        for take, give in zip(takes, gives):
            take.wait()
            give.start()
        for give in gives:
            give.wait()

    hbm = pl.BlockSpec(memory_space=pl.ANY)
    return pl.pallas_call(
        copies,
        out_shape=outs,
        in_specs=[hbm] * count,
        out_specs=(hbm,) * count,
        scratch_shapes=[pltpu.VMEM(out.shape, BF16) for out in outs] + [pltpu.SemaphoreType.DMA((2, count))],
        compiler_params=pltpu.CompilerParams(vmem_limit_bytes=63 * 1024 * 1024),
        cost_estimate=pl.CostEstimate(flops=0, bytes_accessed=2_000_000, transcendentals=0),
    )(*results)


def local(ndp, pair_repr, cotangent, residue_mask, norm_gains, w_proj, w_out, w_up, w_down):
    scale = 1.0 / math.sqrt(ndp * C * C)
    hbm = pl.BlockSpec(memory_space=pl.ANY)
    columns = ROWS * C
    chunks = pltpu.VMEM((PIECES, PEERS, PACK, C), BF16)
    full = pltpu.VMEM((C, columns), F32)
    half = pltpu.VMEM((C, columns), BF16)
    big = pltpu.VMEM((FFN, columns), BF16)
    cube = pltpu.VMEM((1024, C), F32)
    rows_e, rows_f = EARLY // ndp, LATE // ndp
    scratch = [
        pltpu.VMEM((1024, C), BF16), pltpu.VMEM((1, C), jnp.int32), pltpu.VMEM((3, C), F32),
        pltpu.VMEM((4, C, C), BF16), pltpu.VMEM((2, C, C), BF16),
        pltpu.VMEM((C, FFN), BF16), pltpu.VMEM((FFN, C), BF16),
        pltpu.VMEM((1024, C), BF16), pltpu.VMEM((4 * C, C), BF16), pltpu.VMEM((2 * C, C), BF16),
        pltpu.VMEM((C, FFN), BF16), pltpu.VMEM((FFN, C), BF16), pltpu.VMEM((3, C), BF16),
        pltpu.SemaphoreType.DMA((7,)), pltpu.SemaphoreType.DMA((6,)),
        pltpu.VMEM((C, C), F32),
        pltpu.VMEM((3, C, C), F32),
        pltpu.VMEM((4 * C, C), BF16),
        pltpu.VMEM((2, C, C), BF16),
        pltpu.VMEM((FFN, C), BF16),
        pltpu.VMEM((C, FFN), BF16),
        pltpu.VMEM((C, 5 * C), BF16),
        full, half, full, pltpu.VMEM((1, columns), F32), full, full, full, full,
        *([chunks] * 13),
        pltpu.VMEM((PEERS, 64, C), BF16),
        cube, cube, pltpu.VMEM((8, C, C), BF16), pltpu.VMEM((8, C, C), BF16), cube, cube,
        half, big, half, big, full, pltpu.VMEM((5 * C, columns), BF16), half, half,
    ]
    for rows, whole in ((rows_e, EARLY), (rows_f, LATE)):
        scratch += [
            pltpu.VMEM((whole, C), BF16),
            pltpu.VMEM((ndp, rows, C), BF16),
            pltpu.VMEM((rows, C), BF16),
            pltpu.VMEM((PEERS, rows, C), BF16),
            pltpu.VMEM((rows, C), BF16),
            pltpu.VMEM((whole, C), BF16),
        ]
    scratch += [
        pltpu.SemaphoreType.DMA((6,)),
        pltpu.SemaphoreType.DMA((6, PIECES)),
        pltpu.SemaphoreType.DMA((4,)),
        pltpu.SemaphoreType.DMA((2,)),
        pltpu.SemaphoreType.DMA((6,)),
        pltpu.SemaphoreType.DMA((6,)),
    ]
    outs = tuple(
        jax.ShapeDtypeStruct(shape, BF16)
        for shape in ((1024, C), (1024, C), (4 * C, C), (2 * C, C), (C, FFN), (FFN, C), (3, C))
    )
    results = pl.pallas_call(
        functools.partial(kernel, ndp, scale),
        out_shape=outs,
        in_specs=[hbm] * 8,
        out_specs=(hbm,) * 7,
        scratch_shapes=scratch,
        compiler_params=pltpu.CompilerParams(
            collective_id=0, has_side_effects=True, vmem_limit_bytes=63 * 1024 * 1024
        ),
        cost_estimate=pl.CostEstimate(flops=1_600_000_000, bytes_accessed=3_000_000, transcendentals=1_200_000),
    )(
        pair_repr.reshape(1024, C), cotangent.reshape(1024, C), residue_mask, norm_gains, w_proj, w_out, w_up, w_down,
    )
    results = hand_over(outs, results)
    nxt, grad, g_proj, g_out, g_up, g_down, g_gains = results
    return (
        nxt.reshape(1, C, ROWS, C),
        grad.reshape(1, ROWS, C, C),
        g_proj.reshape(4, C, C),
        g_out.reshape(2, C, C),
        g_up,
        g_down,
        g_gains,
    )


def solution(mesh):
    in_specs = (
        P("dp", "dap", None, None),
        P("dp", None, "dap", None),
        P("dp", None),
        P(),
        P(),
        P(),
        P(),
        P(),
    )
    out_specs = (P("dp", None, "dap", None), P("dp", "dap", None, None), P(), P(), P(), P(), P())
    body = functools.partial(local, mesh.shape["dp"])
    return jax.shard_map(body, mesh=mesh, in_specs=in_specs, out_specs=out_specs, check_vma=False)
```

```python
import functools
import math

import jax
import jax.numpy as jnp
from jax import lax
from jax.experimental import pallas as pl
from jax.experimental.pallas import tpu as pltpu
from jax.sharding import PartitionSpec as P

EPSILON = 1e-05
GELU_SCALE = 0.7978845608028654
GELU_CUBIC = 0.044715
MESH = pl.DeviceIdType.MESH
F32 = jnp.float32
BF16 = jnp.bfloat16

C = 128
FFN = 512
ROWS = 8
PEERS = 16
PIECES = 4
PER = ROWS // PIECES
WIDE = PER * C
PACK = PER * 8
PART = PEERS * PER
EARLY = 1536
LATE = 512


AWAY = sorted(
    [(dy, dx) for dy in range(-3, 5) for dx in range(2) if dy or dx],
    key=lambda at: (-abs(at[0]) - 2 * at[1], at[0]),
)


def far_crops(ndp):
    depth = max(1, ndp // 4)
    steps = [(dz, dr) for dz in range(-((depth - 1) // 2), depth // 2 + 1) for dr in range(ndp // depth) if dz or dr]
    return sorted(steps, key=lambda at: (-abs(at[0]) - at[1] // 2, -at[1], at[0]))


def dot(left, right):
    return jnp.dot(left, right, preferred_element_type=F32)


def dot_nt(left, right):
    return lax.dot_general(left, right, (((1,), (1,)), ((), ())), preferred_element_type=F32)


def dot_tn(left, right):
    return lax.dot_general(left, right, (((0,), (0,)), ((), ())), preferred_element_type=F32)


def norm(values):
    average = jnp.sum(values, axis=0, keepdims=True) * (1.0 / C)
    centred = values - average
    inv_std = lax.rsqrt(jnp.sum(centred * centred, axis=0, keepdims=True) * (1.0 / C) + EPSILON)
    return centred * inv_std, inv_std


def norm_back(incoming, normed, inv_std, gain):
    scaled = incoming * gain
    first = jnp.sum(scaled, axis=0, keepdims=True) * (1.0 / C)
    second = jnp.sum(scaled * normed, axis=0, keepdims=True) * (1.0 / C)
    return inv_std * (scaled - first - normed * second)


def wide(block):
    return jnp.concatenate([block] * PER, axis=1) if PER > 1 else block


def split_rows(values):
    parts = [values[:, r * C:(r + 1) * C].reshape(PEERS, 8, C) for r in range(PER)]
    return jnp.concatenate(parts, axis=1) if PER > 1 else parts[0]


def join_rows(chunks):
    parts = [chunks[:, r * 8:(r + 1) * 8, :].reshape(C, C) for r in range(PER)]
    return jnp.concatenate(parts, axis=1) if PER > 1 else parts[0]


def kernel(
    ndp, scale,
    pair_h, cot, mask_h, gains_h, w_proj_h, w_out_h, w_up_h, w_down_h,
    out_next, out_grad_h, out_proj_h, out_out_h, out_up_h, out_down_h, out_gains_h,
    pair, mask_v, gains, w_proj, w_out, w_up, w_down,
    out_grad, out_proj, out_out, out_up, out_down, out_gains, in_sem, out_sem,
    mask_b, gain_b, wpT, woT, wuT, wdT, wcat,
    pairT, lnT, hat0, rstd0, ag, av, bg, bv,
    s_l, r_l, s_r, r_r, s_t, r_t, s_d, r_d, s_dl, r_dl, s_dr, r_dr, s_n, r_c,
    x_p, y_p, x_r, y_r, lc, rc, dc,
    tri_ln, hid, mid_b, mid_ln, d_pre, d_mid, d_stack, d_val, cotT,
    g_e, rs_e, ch_e, ex_e, fin_e, ag_e, g_f, rs_f, ch_f, ex_f, fin_f, ag_f,
    send, recv, once, once_send, red, red_send,
):
    me = lax.axis_index("dap")
    my_dp = lax.axis_index("dp")
    barrier = pltpu.get_barrier_semaphore()

    def peer(dy, dx):
        return lax.rem(me // 2 + dy + 8, 8) * 2 + lax.rem(me + dx, 2)

    depth = max(1, ndp // 4)
    near = ndp // depth
    crops = far_crops(ndp)

    def crop(dz, dr):
        here = lax.rem(my_dp, near)
        if near == 4:
            there = lax.rem(here // 2 + dr // 2, 2) * 2 + lax.rem(here + dr, 2)
        else:
            there = lax.rem(here + dr, near)
        return lax.rem(my_dp // near + dz + depth, depth) * near + there

    for dy, dx in AWAY:
        pl.semaphore_signal(barrier, inc=1, device_id={"dap": peer(dy, dx)}, device_id_type=MESH)
    for dz, dr in crops:
        pl.semaphore_signal(barrier, inc=1, device_id={"dp": crop(dz, dr)}, device_id_type=MESH)

    loads = [
        pltpu.make_async_copy(src, dst, in_sem.at[n])
        for n, (src, dst) in enumerate((
            (pair_h, pair), (mask_h, mask_v), (gains_h, gains), (w_proj_h, w_proj),
            (w_out_h, w_out), (w_up_h, w_up), (w_down_h, w_down),
        ))
    ]
    for load in loads:
        load.start()
    for load in loads[1:4]:
        load.wait()

    mask_k = mask_v[...].astype(F32)
    mask_b[...] = jnp.broadcast_to(mask_k, (C, C)).T
    for n in range(3):
        gain_b[n] = jnp.broadcast_to(gains[n:n + 1, :], (C, C)).T
    for m in range(4):
        w_m = w_proj[m]
        wpT[m * C:(m + 1) * C, :] = w_m.astype(F32).T.astype(BF16)
        wcat[:, m * C:(m + 1) * C] = w_m
    loads[0].wait()

    def exchange(which, src, dst, p):
        for dy, dx in AWAY:
            d = peer(dy, dx)
            pltpu.make_async_remote_copy(
                src_ref=src.at[p, d], dst_ref=dst.at[p, me],
                send_sem=send.at[which], recv_sem=recv.at[which, p],
                device_id={"dap": d}, device_id_type=MESH,
            ).start()
        dst[p, me] = src[p, me]

    def arrived(which, dst, p):
        ref = dst.at[p, pl.ds(0, PEERS - 1)]
        pltpu.make_async_copy(ref, ref, recv.at[which, p]).wait()

    def sent(which, src):
        ref = src.at[:, pl.ds(0, PEERS - 1)]
        pltpu.make_async_copy(ref, ref, send.at[which]).wait()

    def mask_of(p):
        parts = []
        for r in range(PER):
            parts.append(mask_k * mask_b[pl.ds(me * ROWS + p * PER + r, 1), :])
        return jnp.concatenate(parts, axis=1) if PER > 1 else parts[0]

    def columns(p):
        return pl.ds(pl.multiple_of(p * WIDE, WIDE), WIDE)

    def front(p):
        at = columns(p)
        x_rows = pair[at, :].astype(F32)
        x = jnp.concatenate([x_rows[r * C:(r + 1) * C, :].T for r in range(PER)], axis=1) if PER > 1 else x_rows.T
        pairT[:, at] = x
        normed, inv_std = norm(x)
        hat0[:, at] = normed
        rstd0[:, at] = inv_std
        ln = (normed * wide(gain_b[0])).astype(BF16)
        lnT[:, at] = ln
        mask = mask_of(p)
        gate = jax.nn.sigmoid(dot(wpT[0:C, :], ln))
        value = dot(wpT[C:2 * C, :], ln)
        ag[:, at] = gate
        av[:, at] = value
        s_l[p] = split_rows(mask * gate * value).astype(BF16)
        gate = jax.nn.sigmoid(dot(wpT[2 * C:3 * C, :], ln))
        value = dot(wpT[3 * C:4 * C, :], ln)
        bg[:, at] = gate
        bv[:, at] = value
        s_r[p] = split_rows(mask * gate * value).astype(BF16)

    def front_step(p, _):
        exchange(1, s_r, r_r, p)
        front(p + 1)
        return 0

    def send_l(p, _):
        exchange(0, s_l, r_l, p)
        return 0

    front(0)
    pl.semaphore_wait(barrier, PEERS - 1 + ndp - 1)
    lax.fori_loop(0, PIECES - 1, front_step, 0)
    exchange(1, s_r, r_r, PIECES - 1)
    lax.fori_loop(0, PIECES, send_l, 0)

    for dy, dx in AWAY:
        d = peer(dy, dx)
        pltpu.make_async_remote_copy(
            src_ref=cot.at[pl.ds(pl.multiple_of(d * 64, 64), 64)], dst_ref=r_c.at[me],
            send_sem=once_send.at[0], recv_sem=once.at[0],
            device_id={"dap": d}, device_id_type=MESH,
        ).start()
    own_cot = pltpu.make_async_copy(cot.at[pl.ds(pl.multiple_of(me * 64, 64), 64)], r_c.at[me], once.at[1])
    own_cot.start()

    for load in loads[4:]:
        load.wait()
    for m in range(4):
        f_at = slice(m * C, (m + 1) * C)
        wuT[f_at, :] = w_up[:, f_at].astype(F32).T.astype(BF16)
        wdT[:, f_at] = w_down[f_at, :].astype(F32).T.astype(BF16)
    for m in range(2):
        woT[m] = w_out[m].astype(F32).T.astype(BF16)
    wcat[:, 4 * C:5 * C] = w_out[0]
    g_e[1280:EARLY, :] = jnp.zeros((EARLY - 1280, C), BF16)

    def spread(dst, src, p):
        for s in range(PEERS):
            dst[pl.ds(pl.multiple_of(s * 64 + p * PACK, PACK), PACK), :] = src[p, s].astype(F32)

    def gather_chunks(p):
        return lambda ref: jnp.stack(
            [ref[pl.ds(pl.multiple_of(s * 64 + p * PACK, PACK), PACK), :] for s in range(PEERS)]
        ).astype(BF16)

    def take_r(p, _):
        arrived(1, r_r, p)
        spread(x_r, r_r, p)
        return 0

    lax.fori_loop(0, PIECES, take_r, 0)
    for c in range(8):
        rc[c] = x_r[pl.ds(c, C, 8), :].astype(BF16)

    def part(p):
        return pl.ds(pl.multiple_of(p * PART, PART), PART)

    def tri_step(p, _):
        arrived(0, r_l, p)
        x_p[...] = r_l[p].astype(F32).reshape(PEERS * PACK, C)
        for c in range(8):
            left = x_p[pl.ds(c, PART, 8), :].astype(BF16)
            lc[c, part(p), :] = left
            y_p[pl.ds(c, PART, 8), :] = dot_nt(left, rc[c])
        s_t[p] = y_p[...].reshape(PEERS, PACK, C).astype(BF16)
        exchange(2, s_t, r_t, p)
        return 0

    lax.fori_loop(0, PIECES, tri_step, 0)

    own_cot.wait()
    all_cot = r_c.at[pl.ds(0, PEERS - 1)]
    pltpu.make_async_copy(all_cot, all_cot, once.at[0]).wait()

    def next_body(p):
        rows = pl.ds(pl.multiple_of(me * 64 + p * PACK, PACK), PACK)

        for dy, dx in AWAY:
            d = peer(dy, dx)
            pltpu.make_async_remote_copy(
                src_ref=s_n.at[p, d], dst_ref=out_next.at[rows],
                send_sem=once_send.at[1], recv_sem=once.at[2],
                device_id={"dap": d}, device_id_type=MESH,
            ).start()
        pltpu.make_async_copy(s_n.at[p, me], out_next.at[rows], once.at[3]).start()

    def middle(p, _):
        at = columns(p)
        arrived(2, r_t, p)
        tri = join_rows(r_t[p].astype(F32))
        tri_hat, tri_rstd = norm(tri)
        t_ln = (tri_hat * wide(gain_b[1])).astype(BF16)
        tri_ln[:, at] = t_ln
        out_gate = jax.nn.sigmoid(dot(woT[0], lnT[:, at]))
        out_value = dot(woT[1], t_ln)
        mid_r = (pairT[:, at] + out_gate * out_value).astype(BF16)
        mid_b[:, at] = mid_r
        mid = mid_r.astype(F32)
        mid_hat, mid_rstd = norm(mid)
        m_ln = (mid_hat * wide(gain_b[2])).astype(BF16)
        mid_ln[:, at] = m_ln
        cot_rows = r_c[:, pl.ds(pl.multiple_of(p * PACK, PACK), PACK), :].astype(F32)
        cot_t = jnp.concatenate(
            [cot_rows[:, r * 8:(r + 1) * 8, :].reshape(C, C).T for r in range(PER)], axis=1
        )
        cot_b = cot_t.astype(BF16)
        cotT[:, at] = cot_b
        for f in range(4):
            f_at = slice(f * C, (f + 1) * C)
            u = dot(wuT[f_at, :], m_ln)
            square = u * u
            tanh = jnp.tanh(u * (GELU_SCALE + GELU_SCALE * GELU_CUBIC * square))
            half = 0.5 + 0.5 * tanh
            act = u * half
            slope = half + act * (1.0 - tanh) * (GELU_SCALE + 3.0 * GELU_SCALE * GELU_CUBIC * square)
            hid[f_at, at] = act.astype(BF16)
            d_pre[f_at, at] = (dot(w_down[f_at, :], cot_b) * slope).astype(BF16)
        d_mid_v = cot_t + norm_back(dot(w_up[...], d_pre[:, at]), mid_hat, mid_rstd, wide(gain_b[2]))
        d_mid[:, at] = d_mid_v
        d_gate = (d_mid_v * out_value * out_gate * (1.0 - out_gate)).astype(BF16)
        d_stack[4 * C:5 * C, at] = d_gate
        d_value = (d_mid_v * out_gate).astype(BF16)
        d_val[:, at] = d_value
        d_tri = norm_back(dot(w_out[1], d_value), tri_hat, tri_rstd, wide(gain_b[1]))
        s_d[p] = split_rows(d_tri).astype(BF16)
        exchange(3, s_d, r_d, p)
        return 0

    lax.fori_loop(0, PIECES, middle, 0)

    def send_next(p, _):
        at = columns(p)
        nxt = mid_b[:, at].astype(F32) + dot(wdT[...], hid[:, at])
        nxt_rows = jnp.concatenate(
            [nxt[:, r * C:(r + 1) * C].T.reshape(PEERS, 8, C) for r in range(PER)], axis=1
        )
        s_n[p] = nxt_rows.astype(BF16)
        next_body(p)
        return 0

    def reduce_scatter(which, src, dst, rows):
        for dz, dr in crops:
            q = crop(dz, dr)
            pltpu.make_async_remote_copy(
                src_ref=src.at[pl.ds(pl.multiple_of(q * rows, 16), rows)], dst_ref=dst.at[my_dp],
                send_sem=red_send.at[which], recv_sem=red.at[which],
                device_id={"dp": q}, device_id_type=MESH,
            ).start()
        dst[my_dp] = src[pl.ds(pl.multiple_of(my_dp * rows, 16), rows), :]

    def wait_count(ref, sem):
        pltpu.make_async_copy(ref, ref, sem).wait()

    def total(ref, count):
        def body(n, value):
            return value + ref[n].astype(F32)

        return lax.fori_loop(1, count, body, ref[0].astype(F32))

    def cross(which, src, dst):
        for dy, dx in AWAY:
            pltpu.make_async_remote_copy(
                src_ref=src, dst_ref=dst.at[me],
                send_sem=red_send.at[which], recv_sem=red.at[which],
                device_id={"dap": peer(dy, dx)}, device_id_type=MESH,
            ).start()
        dst[me] = src[...]

    def all_gather(which, src, dst, rows):
        place = pl.ds(pl.multiple_of(my_dp * rows, 16), rows)

        for dz, dr in crops:
            pltpu.make_async_remote_copy(
                src_ref=src, dst_ref=dst.at[place],
                send_sem=red_send.at[which], recv_sem=red.at[which],
                device_id={"dp": crop(dz, dr)}, device_id_type=MESH,
            ).start()
        dst[place, :] = src[...]

    rows_e, rows_f = EARLY // ndp, LATE // ndp

    for f in range(4):
        f_at = slice(f * C, (f + 1) * C)
        g_e[f_at, :] = dot_nt(mid_ln[...], d_pre[f_at, :]).astype(BF16)
        g_e[512 + f * C:512 + (f + 1) * C, :] = dot_nt(hid[f_at, :], cotT[...]).astype(BF16)
    g_e[1024:1152, :] = dot_nt(lnT[...], d_stack[4 * C:5 * C, :]).astype(BF16)
    g_e[1152:1280, :] = dot_nt(tri_ln[...], d_val[...]).astype(BF16)
    reduce_scatter(0, g_e, rs_e, rows_e)

    def back_step(p, _):
        arrived(3, r_d, p)
        x_p[...] = r_d[p].astype(F32).reshape(PEERS * PACK, C)
        for c in range(8):
            grad = x_p[pl.ds(c, PART, 8), :].astype(BF16)
            dc[c, part(p), :] = grad
            y_p[pl.ds(c, PART, 8), :] = dot(grad, rc[c])
        s_dl[p] = y_p[...].reshape(PEERS, PACK, C).astype(BF16)
        exchange(4, s_dl, r_dl, p)
        return 0

    lax.fori_loop(0, PIECES, back_step, 0)

    for c in range(8):
        y_r[pl.ds(c, C, 8), :] = dot_tn(dc[c], lc[c])

    def back_right(p, _):
        s_dr[p] = gather_chunks(p)(y_r)
        exchange(5, s_dr, r_dr, p)
        return 0

    lax.fori_loop(0, PIECES, back_right, 0)
    lax.fori_loop(0, PIECES, send_next, 0)

    wait_count(rs_e.at[pl.ds(0, ndp - 1)], red.at[0])
    ch_e[...] = total(rs_e, ndp).astype(BF16)
    cross(1, ch_e, ex_e)

    def lower_left(p, _):
        at = columns(p)
        arrived(4, r_dl, p)
        grad = join_rows(r_dl[p].astype(F32)) * mask_of(p)
        gate = ag[:, at]
        with_gate = grad * gate
        d_stack[0:C, at] = (with_gate * av[:, at] * (1.0 - gate)).astype(BF16)
        d_stack[C:2 * C, at] = with_gate.astype(BF16)
        return 0

    def lower_right(p, _):
        at = columns(p)
        arrived(5, r_dr, p)
        grad = join_rows(r_dr[p].astype(F32)) * mask_of(p)
        gate = bg[:, at]
        with_gate = grad * gate
        d_stack[2 * C:3 * C, at] = (with_gate * bv[:, at] * (1.0 - gate)).astype(BF16)
        d_stack[3 * C:4 * C, at] = with_gate.astype(BF16)
        return 0

    def late_grads(first):
        for m in (first, first + 1):
            m_at = slice(m * C, (m + 1) * C)
            g_f[m_at, :] = dot_nt(lnT[...], d_stack[m_at, :]).astype(BF16)

    lax.fori_loop(0, PIECES, lower_left, 0)
    late_grads(0)
    lax.fori_loop(0, PIECES, lower_right, 0)
    late_grads(2)
    reduce_scatter(2, g_f, rs_f, rows_f)

    def put(n, src, dst):
        copy = pltpu.make_async_copy(src, dst, out_sem.at[n])
        copy.start()
        return copy

    def finish(p, _):
        at = columns(p)
        d_ln = dot(wcat[...], d_stack[:, at])
        result = d_mid[:, at] + norm_back(d_ln, hat0[:, at], rstd0[:, at], wide(gain_b[0]))
        for r in range(PER):
            row = pl.ds(pl.multiple_of(p * WIDE + r * C, C), C)
            out_grad[row, :] = result[:, r * C:(r + 1) * C].T.astype(BF16)
        return 0

    lax.fori_loop(0, PIECES, finish, 0)
    puts = [put(0, out_grad, out_grad_h)]

    wait_count(ex_e.at[pl.ds(0, PEERS - 1)], red.at[1])
    fin_e[...] = (total(ex_e, PEERS) * scale).astype(BF16)
    all_gather(4, fin_e, ag_e, rows_e)

    wait_count(rs_f.at[pl.ds(0, ndp - 1)], red.at[2])
    ch_f[...] = total(rs_f, ndp).astype(BF16)
    cross(3, ch_f, ex_f)
    wait_count(ex_f.at[pl.ds(0, PEERS - 1)], red.at[3])
    fin_f[...] = (total(ex_f, PEERS) * scale).astype(BF16)
    all_gather(5, fin_f, ag_f, rows_f)

    wait_count(ag_e.at[pl.ds(0, (ndp - 1) * rows_e)], red.at[4])
    mid_sum = jnp.zeros((C, C), F32)
    for f in range(4):
        f_at = slice(f * C, (f + 1) * C)
        block = ag_e[f_at, :]
        out_up[:, f_at] = block
        mid_sum = mid_sum + block.astype(F32) * w_up[:, f_at].astype(F32)
    out_down[...] = ag_e[512:1024, :]
    out_out[...] = ag_e[1024:1280, :]
    puts += [put(1, out_up, out_up_h), put(2, out_down, out_down_h), put(3, out_out, out_out_h)]
    pair_sum = ag_e[1024:1152, :].astype(F32) * w_out[0].astype(F32)
    tri_sum = ag_e[1152:1280, :].astype(F32) * w_out[1].astype(F32)

    wait_count(ag_f.at[pl.ds(0, (ndp - 1) * rows_f)], red.at[5])
    for m in range(4):
        block = ag_f[m * C:(m + 1) * C, :]
        pair_sum = pair_sum + block.astype(F32) * w_proj[m].astype(F32)
    out_proj[...] = ag_f[...]
    sums = [jnp.sum(s.T, axis=0, keepdims=True) for s in (pair_sum, tri_sum, mid_sum)]
    out_gains[...] = (jnp.concatenate(sums, axis=0) / gains[...]).astype(BF16)
    puts += [put(4, out_proj, out_proj_h), put(5, out_gains, out_gains_h)]

    for copy in puts:
        copy.wait()
    for which, src in enumerate((s_l, s_r, s_t, s_d, s_dl, s_dr)):
        sent(which, src)
    sent_cot = r_c.at[pl.ds(0, PEERS - 1)]
    wait_count(sent_cot, once_send.at[0])
    all_next = s_n.at[:, pl.ds(0, PEERS - 1)]
    wait_count(all_next, once_send.at[1])
    wait_count(all_next, once.at[2])
    wait_count(s_n.at[:, 0], once.at[3])
    wait_count(rs_e.at[pl.ds(0, ndp - 1)], red_send.at[0])
    wait_count(ex_e.at[pl.ds(0, PEERS - 1)], red_send.at[1])
    wait_count(rs_f.at[pl.ds(0, ndp - 1)], red_send.at[2])
    wait_count(ex_f.at[pl.ds(0, PEERS - 1)], red_send.at[3])
    wait_count(ag_e.at[pl.ds(0, (ndp - 1) * rows_e)], red_send.at[4])
    wait_count(ag_f.at[pl.ds(0, (ndp - 1) * rows_f)], red_send.at[5])


def hand_over(outs, results):
    count = len(outs)

    def copies(*refs):
        held = refs[2 * count:3 * count]
        sems = refs[3 * count]
        takes = [pltpu.make_async_copy(refs[n], held[n], sems.at[0, n]) for n in range(count)]
        gives = [pltpu.make_async_copy(held[n], refs[count + n], sems.at[1, n]) for n in range(count)]
        for take in takes:
            take.start()
        for take, give in zip(takes, gives):
            take.wait()
            give.start()
        for give in gives:
            give.wait()

    hbm = pl.BlockSpec(memory_space=pl.ANY)
    return pl.pallas_call(
        copies,
        out_shape=outs,
        in_specs=[hbm] * count,
        out_specs=(hbm,) * count,
        scratch_shapes=[pltpu.VMEM(out.shape, BF16) for out in outs] + [pltpu.SemaphoreType.DMA((2, count))],
        compiler_params=pltpu.CompilerParams(vmem_limit_bytes=63 * 1024 * 1024),
        cost_estimate=pl.CostEstimate(flops=0, bytes_accessed=2_000_000, transcendentals=0),
    )(*results)


def local(ndp, pair_repr, cotangent, residue_mask, norm_gains, w_proj, w_out, w_up, w_down):
    scale = 1.0 / math.sqrt(ndp * C * C)
    hbm = pl.BlockSpec(memory_space=pl.ANY)
    columns = ROWS * C
    chunks = pltpu.VMEM((PIECES, PEERS, PACK, C), BF16)
    full = pltpu.VMEM((C, columns), F32)
    half = pltpu.VMEM((C, columns), BF16)
    big = pltpu.VMEM((FFN, columns), BF16)
    cube = pltpu.VMEM((1024, C), F32)
    rows_e, rows_f = EARLY // ndp, LATE // ndp
    scratch = [
        pltpu.VMEM((1024, C), BF16), pltpu.VMEM((1, C), jnp.int32), pltpu.VMEM((3, C), F32),
        pltpu.VMEM((4, C, C), BF16), pltpu.VMEM((2, C, C), BF16),
        pltpu.VMEM((C, FFN), BF16), pltpu.VMEM((FFN, C), BF16),
        pltpu.VMEM((1024, C), BF16), pltpu.VMEM((4 * C, C), BF16), pltpu.VMEM((2 * C, C), BF16),
        pltpu.VMEM((C, FFN), BF16), pltpu.VMEM((FFN, C), BF16), pltpu.VMEM((3, C), BF16),
        pltpu.SemaphoreType.DMA((7,)), pltpu.SemaphoreType.DMA((6,)),
        pltpu.VMEM((C, C), F32),
        pltpu.VMEM((3, C, C), F32),
        pltpu.VMEM((4 * C, C), BF16),
        pltpu.VMEM((2, C, C), BF16),
        pltpu.VMEM((FFN, C), BF16),
        pltpu.VMEM((C, FFN), BF16),
        pltpu.VMEM((C, 5 * C), BF16),
        full, half, full, pltpu.VMEM((1, columns), F32), full, full, full, full,
        *([chunks] * 13),
        pltpu.VMEM((PEERS, 64, C), BF16),
        pltpu.VMEM((PEERS * PACK, C), F32), pltpu.VMEM((PEERS * PACK, C), F32), cube, cube,
        *([pltpu.VMEM((8, C, C), BF16)] * 3),
        half, big, half, half, big, full, pltpu.VMEM((5 * C, columns), BF16), half, half,
    ]
    for rows, whole in ((rows_e, EARLY), (rows_f, LATE)):
        scratch += [
            pltpu.VMEM((whole, C), BF16),
            pltpu.VMEM((ndp, rows, C), BF16),
            pltpu.VMEM((rows, C), BF16),
            pltpu.VMEM((PEERS, rows, C), BF16),
            pltpu.VMEM((rows, C), BF16),
            pltpu.VMEM((whole, C), BF16),
        ]
    scratch += [
        pltpu.SemaphoreType.DMA((6,)),
        pltpu.SemaphoreType.DMA((6, PIECES)),
        pltpu.SemaphoreType.DMA((4,)),
        pltpu.SemaphoreType.DMA((2,)),
        pltpu.SemaphoreType.DMA((6,)),
        pltpu.SemaphoreType.DMA((6,)),
    ]
    outs = tuple(
        jax.ShapeDtypeStruct(shape, BF16)
        for shape in ((1024, C), (1024, C), (4 * C, C), (2 * C, C), (C, FFN), (FFN, C), (3, C))
    )
    results = pl.pallas_call(
        functools.partial(kernel, ndp, scale),
        out_shape=outs,
        in_specs=[hbm] * 8,
        out_specs=(hbm,) * 7,
        scratch_shapes=scratch,
        compiler_params=pltpu.CompilerParams(
            collective_id=0, has_side_effects=True, vmem_limit_bytes=63 * 1024 * 1024
        ),
        cost_estimate=pl.CostEstimate(flops=1_600_000_000, bytes_accessed=3_000_000, transcendentals=1_200_000),
    )(
        pair_repr.reshape(1024, C), cotangent.reshape(1024, C), residue_mask, norm_gains, w_proj, w_out, w_up, w_down,
    )
    results = hand_over(outs, results)
    nxt, grad, g_proj, g_out, g_up, g_down, g_gains = results
    return (
        nxt.reshape(1, C, ROWS, C),
        grad.reshape(1, ROWS, C, C),
        g_proj.reshape(4, C, C),
        g_out.reshape(2, C, C),
        g_up,
        g_down,
        g_gains,
    )


def solution(mesh):
    in_specs = (
        P("dp", "dap", None, None),
        P("dp", None, "dap", None),
        P("dp", None),
        P(),
        P(),
        P(),
        P(),
        P(),
    )
    out_specs = (P("dp", None, "dap", None), P("dp", "dap", None, None), P(), P(), P(), P(), P())
    body = functools.partial(local, mesh.shape["dp"])
    return jax.shard_map(body, mesh=mesh, in_specs=in_specs, out_specs=out_specs, check_vma=False)
```

```python
import functools
import math

import jax
import jax.numpy as jnp
from jax import lax
from jax.experimental import pallas as pl
from jax.experimental.pallas import tpu as pltpu
from jax.sharding import PartitionSpec as P

EPSILON = 1e-05
GELU_SCALE = 0.7978845608028654
GELU_CUBIC = 0.044715
MESH = pl.DeviceIdType.MESH
F32 = jnp.float32
BF16 = jnp.bfloat16

C = 128
FFN = 512
ROWS = 8
PEERS = 16
PIECES = 4
PER = ROWS // PIECES
WIDE = PER * C
PACK = PER * 8
PART = PEERS * PER
EARLY = 1536
LATE = 512


AWAY = sorted(
    [(dy, dx) for dy in range(-3, 5) for dx in range(2) if dy or dx],
    key=lambda at: (-abs(at[0]) - 2 * at[1], at[0]),
)


def far_crops(ndp):
    depth = max(1, ndp // 4)
    steps = [(dz, dr) for dz in range(-((depth - 1) // 2), depth // 2 + 1) for dr in range(ndp // depth) if dz or dr]
    return sorted(steps, key=lambda at: (-abs(at[0]) - at[1] // 2, -at[1], at[0]))


def dot(left, right):
    return jnp.dot(left, right, preferred_element_type=F32)


def dot_nt(left, right):
    return lax.dot_general(left, right, (((1,), (1,)), ((), ())), preferred_element_type=F32)


def dot_tn(left, right):
    return lax.dot_general(left, right, (((0,), (0,)), ((), ())), preferred_element_type=F32)


def norm(values):
    average = jnp.sum(values, axis=0, keepdims=True) * (1.0 / C)
    centred = values - average
    inv_std = lax.rsqrt(jnp.sum(centred * centred, axis=0, keepdims=True) * (1.0 / C) + EPSILON)
    return centred * inv_std, inv_std


def norm_back(incoming, normed, inv_std, gain):
    scaled = incoming * gain
    first = jnp.sum(scaled, axis=0, keepdims=True) * (1.0 / C)
    second = jnp.sum(scaled * normed, axis=0, keepdims=True) * (1.0 / C)
    return inv_std * (scaled - first - normed * second)


def wide(block):
    return jnp.concatenate([block] * PER, axis=1) if PER > 1 else block


def split_rows(values):
    parts = [values[:, r * C:(r + 1) * C].reshape(PEERS, 8, C) for r in range(PER)]
    return jnp.concatenate(parts, axis=1) if PER > 1 else parts[0]


def join_rows(chunks):
    parts = [chunks[:, r * 8:(r + 1) * 8, :].reshape(C, C) for r in range(PER)]
    return jnp.concatenate(parts, axis=1) if PER > 1 else parts[0]


def kernel(
    ndp, scale,
    pair_h, cot, mask_h, gains_h, w_proj_h, w_out_h, w_up_h, w_down_h,
    out_next, out_grad, out_proj, out_out, out_up, out_down, out_gains,
    pair, mask_v, gains, w_proj, w_out, w_up, w_down, in_sem,
    mask_b, gain_b, wpT, woT, wuT, wdT, wcat,
    pairT, lnT, hat0, rstd0, ag, av, bg, bv,
    s_l, r_l, s_r, r_r, s_t, r_t, s_d, r_d, s_dl, r_dl, s_dr, r_dr, s_n, r_c,
    x_p, y_p, x_r, y_r, lc, rc, dc,
    tri_ln, hid, mid_b, mid_ln, d_pre, d_mid, d_stack, d_val, cotT,
    g_e, sib_e, half_e, rs_e, ch_e, ex_e, fin_e, ag_e, g_f, rs_f, ch_f, ex_f, fin_f, ag_f,
    send, recv, once, once_send, red, red_send,
):
    me = lax.axis_index("dap")
    my_dp = lax.axis_index("dp")
    barrier = pltpu.get_barrier_semaphore()

    def peer(dy, dx):
        return lax.rem(me // 2 + dy + 8, 8) * 2 + lax.rem(me + dx, 2)

    depth = max(1, ndp // 4)
    near = ndp // depth
    crops = far_crops(ndp)

    def crop(dz, dr):
        here = lax.rem(my_dp, near)
        if near == 4:
            there = lax.rem(here // 2 + dr // 2, 2) * 2 + lax.rem(here + dr, 2)
        else:
            there = lax.rem(here + dr, near)
        return lax.rem(my_dp // near + dz + depth, depth) * near + there

    for dy, dx in AWAY:
        pl.semaphore_signal(barrier, inc=1, device_id={"dap": peer(dy, dx)}, device_id_type=MESH)
    for dz, dr in crops:
        pl.semaphore_signal(barrier, inc=1, device_id={"dp": crop(dz, dr)}, device_id_type=MESH)

    loads = [
        pltpu.make_async_copy(src, dst, in_sem.at[n])
        for n, (src, dst) in enumerate((
            (pair_h, pair), (mask_h, mask_v), (gains_h, gains), (w_proj_h, w_proj),
            (w_out_h, w_out), (w_up_h, w_up), (w_down_h, w_down),
        ))
    ]
    for load in loads:
        load.start()
    for load in loads[1:4]:
        load.wait()

    mask_k = mask_v[...].astype(F32)
    mask_b[...] = jnp.broadcast_to(mask_k, (C, C)).T
    for n in range(3):
        gain_b[n] = jnp.broadcast_to(gains[n:n + 1, :], (C, C)).T
    for m in range(4):
        w_m = w_proj[m]
        wpT[m * C:(m + 1) * C, :] = w_m.astype(F32).T.astype(BF16)
        wcat[:, m * C:(m + 1) * C] = w_m
    loads[0].wait()

    def exchange(which, src, dst, p):
        for dy, dx in AWAY:
            d = peer(dy, dx)
            pltpu.make_async_remote_copy(
                src_ref=src.at[p, d], dst_ref=dst.at[p, me],
                send_sem=send.at[which], recv_sem=recv.at[which, p],
                device_id={"dap": d}, device_id_type=MESH,
            ).start()
        dst[p, me] = src[p, me]

    def arrived(which, dst, p):
        ref = dst.at[p, pl.ds(0, PEERS - 1)]
        pltpu.make_async_copy(ref, ref, recv.at[which, p]).wait()

    def sent(which, src):
        ref = src.at[:, pl.ds(0, PEERS - 1)]
        pltpu.make_async_copy(ref, ref, send.at[which]).wait()

    def mask_of(p):
        parts = []
        for r in range(PER):
            parts.append(mask_k * mask_b[pl.ds(me * ROWS + p * PER + r, 1), :])
        return jnp.concatenate(parts, axis=1) if PER > 1 else parts[0]

    def columns(p):
        return pl.ds(pl.multiple_of(p * WIDE, WIDE), WIDE)

    def front(p):
        at = columns(p)
        x_rows = pair[at, :].astype(F32)
        x = jnp.concatenate([x_rows[r * C:(r + 1) * C, :].T for r in range(PER)], axis=1) if PER > 1 else x_rows.T
        pairT[:, at] = x
        normed, inv_std = norm(x)
        hat0[:, at] = normed
        rstd0[:, at] = inv_std
        ln = (normed * wide(gain_b[0])).astype(BF16)
        lnT[:, at] = ln
        mask = mask_of(p)
        gate = jax.nn.sigmoid(dot(wpT[0:C, :], ln))
        value = dot(wpT[C:2 * C, :], ln)
        ag[:, at] = gate
        av[:, at] = value
        s_l[p] = split_rows(mask * gate * value).astype(BF16)
        gate = jax.nn.sigmoid(dot(wpT[2 * C:3 * C, :], ln))
        value = dot(wpT[3 * C:4 * C, :], ln)
        bg[:, at] = gate
        bv[:, at] = value
        s_r[p] = split_rows(mask * gate * value).astype(BF16)

    def front_step(p, _):
        exchange(1, s_r, r_r, p)
        front(p + 1)
        return 0

    def send_l(p, _):
        exchange(0, s_l, r_l, p)
        return 0

    front(0)
    pl.semaphore_wait(barrier, PEERS - 1 + ndp - 1)
    lax.fori_loop(0, PIECES - 1, front_step, 0)
    exchange(1, s_r, r_r, PIECES - 1)
    lax.fori_loop(0, PIECES, send_l, 0)

    own_cot = pltpu.make_async_copy(cot.at[pl.ds(pl.multiple_of(me * 64, 64), 64)], r_c.at[me], once.at[0])
    own_cot.start()

    def send_cot(p):
        here = pl.ds(pl.multiple_of(p * PACK, PACK), PACK)
        for dy, dx in AWAY:
            d = peer(dy, dx)
            pltpu.make_async_remote_copy(
                src_ref=cot.at[pl.ds(pl.multiple_of(d * 64 + p * PACK, PACK), PACK)], dst_ref=r_c.at[me, here],
                send_sem=once_send.at[0], recv_sem=recv.at[6, p],
                device_id={"dap": d}, device_id_type=MESH,
            ).start()

    for load in loads[4:]:
        load.wait()
    for m in range(4):
        f_at = slice(m * C, (m + 1) * C)
        wuT[f_at, :] = w_up[:, f_at].astype(F32).T.astype(BF16)
        wdT[:, f_at] = w_down[f_at, :].astype(F32).T.astype(BF16)
    for m in range(2):
        woT[m] = w_out[m].astype(F32).T.astype(BF16)
    wcat[:, 4 * C:5 * C] = w_out[0]
    g_e[1280:EARLY, :] = jnp.zeros((EARLY - 1280, C), BF16)

    def spread(dst, src, p):
        for s in range(PEERS):
            dst[pl.ds(pl.multiple_of(s * 64 + p * PACK, PACK), PACK), :] = src[p, s].astype(F32)

    def gather_chunks(p):
        return lambda ref: jnp.stack(
            [ref[pl.ds(pl.multiple_of(s * 64 + p * PACK, PACK), PACK), :] for s in range(PEERS)]
        ).astype(BF16)

    def take_r(p, _):
        arrived(1, r_r, p)
        spread(x_r, r_r, p)
        return 0

    lax.fori_loop(0, PIECES, take_r, 0)
    for c in range(8):
        rc[c] = x_r[pl.ds(c, C, 8), :].astype(BF16)

    def part(p):
        return pl.ds(pl.multiple_of(p * PART, PART), PART)

    def tri_step(p, _):
        arrived(0, r_l, p)
        x_p[...] = r_l[p].astype(F32).reshape(PEERS * PACK, C)
        for c in range(8):
            left = x_p[pl.ds(c, PART, 8), :].astype(BF16)
            lc[c, part(p), :] = left
            y_p[pl.ds(c, PART, 8), :] = dot_nt(left, rc[c])
        s_t[p] = y_p[...].reshape(PEERS, PACK, C).astype(BF16)
        exchange(2, s_t, r_t, p)
        send_cot(p)
        return 0

    lax.fori_loop(0, PIECES, tri_step, 0)

    own_cot.wait()

    def next_body(p):
        rows = pl.ds(pl.multiple_of(me * 64 + p * PACK, PACK), PACK)

        for dy, dx in AWAY:
            d = peer(dy, dx)
            pltpu.make_async_remote_copy(
                src_ref=s_n.at[p, d], dst_ref=out_next.at[rows],
                send_sem=once_send.at[1], recv_sem=once.at[2],
                device_id={"dap": d}, device_id_type=MESH,
            ).start()
        pltpu.make_async_copy(s_n.at[p, me], out_next.at[rows], once.at[3]).start()

    def middle(p, _):
        at = columns(p)
        arrived(2, r_t, p)
        tri = join_rows(r_t[p].astype(F32))
        tri_hat, tri_rstd = norm(tri)
        t_ln = (tri_hat * wide(gain_b[1])).astype(BF16)
        tri_ln[:, at] = t_ln
        out_gate = jax.nn.sigmoid(dot(woT[0], lnT[:, at]))
        out_value = dot(woT[1], t_ln)
        mid_r = (pairT[:, at] + out_gate * out_value).astype(BF16)
        mid_b[:, at] = mid_r
        mid = mid_r.astype(F32)
        mid_hat, mid_rstd = norm(mid)
        m_ln = (mid_hat * wide(gain_b[2])).astype(BF16)
        mid_ln[:, at] = m_ln
        cot_piece = r_c.at[pl.ds(0, PEERS - 1), pl.ds(0, PACK)]
        pltpu.make_async_copy(cot_piece, cot_piece, recv.at[6, p]).wait()
        cot_rows = r_c[:, pl.ds(pl.multiple_of(p * PACK, PACK), PACK), :].astype(F32)
        cot_t = jnp.concatenate(
            [cot_rows[:, r * 8:(r + 1) * 8, :].reshape(C, C).T for r in range(PER)], axis=1
        )
        cot_b = cot_t.astype(BF16)
        cotT[:, at] = cot_b
        for f in range(4):
            f_at = slice(f * C, (f + 1) * C)
            u = dot(wuT[f_at, :], m_ln)
            square = u * u
            tanh = jnp.tanh(u * (GELU_SCALE + GELU_SCALE * GELU_CUBIC * square))
            half = 0.5 + 0.5 * tanh
            act = u * half
            slope = half + act * (1.0 - tanh) * (GELU_SCALE + 3.0 * GELU_SCALE * GELU_CUBIC * square)
            hid[f_at, at] = act.astype(BF16)
            d_pre[f_at, at] = (dot(w_down[f_at, :], cot_b) * slope).astype(BF16)
        d_mid_v = cot_t + norm_back(dot(w_up[...], d_pre[:, at]), mid_hat, mid_rstd, wide(gain_b[2]))
        d_mid[:, at] = d_mid_v
        d_gate = (d_mid_v * out_value * out_gate * (1.0 - out_gate)).astype(BF16)
        d_stack[4 * C:5 * C, at] = d_gate
        d_value = (d_mid_v * out_gate).astype(BF16)
        d_val[:, at] = d_value
        d_tri = norm_back(dot(w_out[1], d_value), tri_hat, tri_rstd, wide(gain_b[1]))
        s_d[p] = split_rows(d_tri).astype(BF16)
        exchange(3, s_d, r_d, p)
        return 0

    lax.fori_loop(0, PIECES, middle, 0)

    def send_next(p, _):
        at = columns(p)
        nxt = mid_b[:, at].astype(F32) + dot(wdT[...], hid[:, at])
        nxt_rows = jnp.concatenate(
            [nxt[:, r * C:(r + 1) * C].T.reshape(PEERS, 8, C) for r in range(PER)], axis=1
        )
        s_n[p] = nxt_rows.astype(BF16)
        next_body(p)
        return 0

    rows_e, rows_f = EARLY // ndp, LATE // ndp

    core = lax.rem(my_dp, 2)
    place_dp = my_dp // 2
    places = ndp // 2
    sibling = {"dp": place_dp * 2 + 1 - core}
    half_rows = EARLY // 2

    def core_half(which):
        return pl.ds(pl.multiple_of(which * half_rows, 16), half_rows)

    chips = [(dz, dr) for dz, dr in crops if dr % 2 == 0]

    def chip(dz, dr):
        return crop(dz, dr) // 2

    def spread_early():
        for dz, dr in chips:
            q = chip(dz, dr)
            pltpu.make_async_remote_copy(
                src_ref=half_e.at[pl.ds(pl.multiple_of(q * rows_e, 16), rows_e)], dst_ref=rs_e.at[place_dp],
                send_sem=red_send.at[0], recv_sem=red.at[0],
                device_id={"dp": q * 2 + core}, device_id_type=MESH,
            ).start()
        rs_e[place_dp] = half_e[pl.ds(pl.multiple_of(place_dp * rows_e, 16), rows_e), :]

    def gather_early():
        place = pl.ds(pl.multiple_of(core * half_rows + place_dp * rows_e, 16), rows_e)
        for dz, dr in chips:
            pltpu.make_async_remote_copy(
                src_ref=fin_e, dst_ref=ag_e.at[place],
                send_sem=red_send.at[4], recv_sem=red.at[4],
                device_id={"dp": chip(dz, dr) * 2 + core}, device_id_type=MESH,
            ).start()
        ag_e[place, :] = fin_e[...]

    def spread_late(side):
        target = 1 - side
        for dz, dr in chips:
            q = chip(dz, dr)
            pltpu.make_async_remote_copy(
                src_ref=g_f.at[pl.ds(pl.multiple_of(side * 2 * C + q * rows_f, 16), rows_f)], dst_ref=rs_f.at[my_dp],
                send_sem=red_send.at[2], recv_sem=red.at[2],
                device_id={"dp": q * 2 + target}, device_id_type=MESH,
            ).start()
        own = pl.ds(pl.multiple_of(side * 2 * C + place_dp * rows_f, 16), rows_f)

        @pl.when(core == target)
        def _():
            rs_f[my_dp] = g_f[own, :]

        @pl.when(core != target)
        def _():
            pltpu.make_async_remote_copy(
                src_ref=g_f.at[own], dst_ref=rs_f.at[my_dp],
                send_sem=red_send.at[2], recv_sem=red.at[2],
                device_id=sibling, device_id_type=MESH,
            ).start()

    def wait_count(ref, sem):
        pltpu.make_async_copy(ref, ref, sem).wait()

    def total(ref):
        return jnp.sum(ref[...].astype(F32), axis=0)

    def cross(which, src, dst):
        for dy, dx in AWAY:
            pltpu.make_async_remote_copy(
                src_ref=src, dst_ref=dst.at[me],
                send_sem=red_send.at[which], recv_sem=red.at[which],
                device_id={"dap": peer(dy, dx)}, device_id_type=MESH,
            ).start()
        dst[me] = src[...]

    def gather_late(which, src, dst, rows):
        place = pl.ds(pl.multiple_of((1 - core) * 2 * C + place_dp * rows, 16), rows)

        for dz, dr in crops:
            pltpu.make_async_remote_copy(
                src_ref=src, dst_ref=dst.at[place],
                send_sem=red_send.at[which], recv_sem=red.at[which],
                device_id={"dp": crop(dz, dr)}, device_id_type=MESH,
            ).start()
        dst[place, :] = src[...]

    for f in range(4):
        f_at = slice(f * C, (f + 1) * C)
        g_e[f_at, :] = dot_nt(mid_ln[...], d_pre[f_at, :]).astype(BF16)
        g_e[512 + f * C:512 + (f + 1) * C, :] = dot_nt(hid[f_at, :], cotT[...]).astype(BF16)
    g_e[1024:1152, :] = dot_nt(lnT[...], d_stack[4 * C:5 * C, :]).astype(BF16)
    g_e[1152:1280, :] = dot_nt(tri_ln[...], d_val[...]).astype(BF16)
    add_cores = pltpu.make_async_remote_copy(
        src_ref=g_e.at[core_half(1 - core)], dst_ref=sib_e,
        send_sem=red_send.at[1], recv_sem=red.at[6],
        device_id=sibling, device_id_type=MESH,
    )
    add_cores.start()

    def back_step(p, _):
        arrived(3, r_d, p)
        x_p[...] = r_d[p].astype(F32).reshape(PEERS * PACK, C)
        for c in range(8):
            grad = x_p[pl.ds(c, PART, 8), :].astype(BF16)
            dc[c, part(p), :] = grad
            y_p[pl.ds(c, PART, 8), :] = dot(grad, rc[c])
        s_dl[p] = y_p[...].reshape(PEERS, PACK, C).astype(BF16)
        exchange(4, s_dl, r_dl, p)
        return 0

    back_step(0, 0)
    add_cores.wait_recv()
    half_e[...] = (g_e[core_half(core), :].astype(F32) + sib_e[...].astype(F32)).astype(BF16)
    spread_early()
    lax.fori_loop(1, PIECES, back_step, 0)

    for c in range(8):
        y_r[pl.ds(c, C, 8), :] = dot_tn(dc[c], lc[c])

    def back_right(p, _):
        s_dr[p] = gather_chunks(p)(y_r)
        exchange(5, s_dr, r_dr, p)
        return 0

    lax.fori_loop(0, PIECES, back_right, 0)
    lax.fori_loop(0, PIECES, send_next, 0)

    def lower_left(p, _):
        at = columns(p)
        arrived(4, r_dl, p)
        grad = join_rows(r_dl[p].astype(F32)) * mask_of(p)
        gate = ag[:, at]
        with_gate = grad * gate
        d_stack[0:C, at] = (with_gate * av[:, at] * (1.0 - gate)).astype(BF16)
        d_stack[C:2 * C, at] = with_gate.astype(BF16)
        return 0

    def lower_right(p, _):
        at = columns(p)
        arrived(5, r_dr, p)
        grad = join_rows(r_dr[p].astype(F32)) * mask_of(p)
        gate = bg[:, at]
        with_gate = grad * gate
        d_stack[2 * C:3 * C, at] = (with_gate * bv[:, at] * (1.0 - gate)).astype(BF16)
        d_stack[3 * C:4 * C, at] = with_gate.astype(BF16)
        return 0

    def late_grads(first):
        for m in (first, first + 1):
            m_at = slice(m * C, (m + 1) * C)
            g_f[m_at, :] = dot_nt(lnT[...], d_stack[m_at, :]).astype(BF16)

    lax.fori_loop(0, PIECES, lower_left, 0)
    late_grads(0)
    spread_late(0)
    wait_count(rs_e.at[pl.ds(0, places - 1)], red.at[0])
    ch_e[...] = total(rs_e).astype(BF16)
    cross(5, ch_e, ex_e)
    lax.fori_loop(0, PIECES, lower_right, 0)
    late_grads(2)
    spread_late(1)

    def finish(p, _):
        at = columns(p)
        d_ln = dot(wcat[...], d_stack[:, at])
        result = d_mid[:, at] + norm_back(d_ln, hat0[:, at], rstd0[:, at], wide(gain_b[0]))
        for r in range(PER):
            row = pl.ds(pl.multiple_of(p * WIDE + r * C, C), C)
            out_grad[row, :] = result[:, r * C:(r + 1) * C].T.astype(BF16)
        return 0

    lax.fori_loop(0, PIECES, finish, 0)

    wait_count(ex_e.at[pl.ds(0, PEERS - 1)], red.at[5])
    fin_e[...] = (total(ex_e) * scale).astype(BF16)
    gather_early()

    wait_count(rs_f.at[pl.ds(0, ndp - 1)], red.at[2])
    ch_f[...] = total(rs_f).astype(BF16)
    cross(3, ch_f, ex_f)
    wait_count(ex_f.at[pl.ds(0, PEERS - 1)], red.at[3])
    fin_f[...] = (total(ex_f) * scale).astype(BF16)
    gather_late(7, fin_f, ag_f, rows_f)

    wait_count(ag_e.at[pl.ds(0, (places - 1) * rows_e)], red.at[4])
    to_core = pltpu.make_async_remote_copy(
        src_ref=ag_e.at[core_half(core)], dst_ref=ag_e.at[core_half(core)],
        send_sem=red_send.at[6], recv_sem=red.at[1],
        device_id=sibling, device_id_type=MESH,
    )
    to_core.start()
    to_core.wait_recv()
    mid_sum = jnp.zeros((C, C), F32)
    for f in range(4):
        f_at = slice(f * C, (f + 1) * C)
        block = ag_e[f_at, :]
        out_up[:, f_at] = block
        mid_sum = mid_sum + block.astype(F32) * w_up[:, f_at].astype(F32)
    out_down[...] = ag_e[512:1024, :]
    out_out[...] = ag_e[1024:1280, :]
    pair_sum = ag_e[1024:1152, :].astype(F32) * w_out[0].astype(F32)
    tri_sum = ag_e[1152:1280, :].astype(F32) * w_out[1].astype(F32)

    wait_count(ag_f.at[pl.ds(0, (ndp - 1) * rows_f)], red.at[7])
    for m in range(4):
        block = ag_f[m * C:(m + 1) * C, :]
        pair_sum = pair_sum + block.astype(F32) * w_proj[m].astype(F32)
    out_proj[...] = ag_f[...]
    sums = [jnp.sum(s.T, axis=0, keepdims=True) for s in (pair_sum, tri_sum, mid_sum)]
    out_gains[...] = (jnp.concatenate(sums, axis=0) / gains[...]).astype(BF16)

    for which, src in enumerate((s_l, s_r, s_t, s_d, s_dl, s_dr)):
        sent(which, src)
    sent_cot = r_c.at[pl.ds(0, PEERS - 1)]
    wait_count(sent_cot, once_send.at[0])
    all_next = s_n.at[:, pl.ds(0, PEERS - 1)]
    wait_count(all_next, once_send.at[1])
    wait_count(all_next, once.at[2])
    wait_count(s_n.at[:, 0], once.at[3])
    add_cores.wait_send()
    to_core.wait_send()
    wait_count(rs_e.at[pl.ds(0, places - 1)], red_send.at[0])
    wait_count(ex_e.at[pl.ds(0, PEERS - 1)], red_send.at[5])
    wait_count(rs_f.at[pl.ds(0, ndp - 1)], red_send.at[2])
    wait_count(ex_f.at[pl.ds(0, PEERS - 1)], red_send.at[3])
    wait_count(ag_e.at[pl.ds(0, (places - 1) * rows_e)], red_send.at[4])
    wait_count(ag_f.at[pl.ds(0, (ndp - 1) * rows_f)], red_send.at[7])


def hand_over(outs, results):
    count = len(outs)

    def copies(*refs):
        sems = refs[2 * count]
        gives = [pltpu.make_async_copy(refs[n], refs[count + n], sems.at[n]) for n in range(count)]
        for give in gives:
            give.start()
        for give in gives:
            give.wait()

    return pl.pallas_call(
        copies,
        out_shape=outs,
        in_specs=[pl.BlockSpec(memory_space=pltpu.VMEM)] * count,
        out_specs=(pl.BlockSpec(memory_space=pltpu.HBM),) * count,
        scratch_shapes=[pltpu.SemaphoreType.DMA((count,))],
        compiler_params=pltpu.CompilerParams(vmem_limit_bytes=48 * 1024 * 1024),
        cost_estimate=pl.CostEstimate(flops=0, bytes_accessed=2_000_000, transcendentals=0),
    )(*results)


def local(ndp, pair_repr, cotangent, residue_mask, norm_gains, w_proj, w_out, w_up, w_down):
    scale = 1.0 / math.sqrt(ndp * C * C)
    hbm = pl.BlockSpec(memory_space=pltpu.HBM)
    vmem = pl.BlockSpec(memory_space=pltpu.VMEM)
    columns = ROWS * C
    chunks = pltpu.VMEM((PIECES, PEERS, PACK, C), BF16)
    full = pltpu.VMEM((C, columns), F32)
    half = pltpu.VMEM((C, columns), BF16)
    big = pltpu.VMEM((FFN, columns), BF16)
    cube = pltpu.VMEM((1024, C), F32)
    rows_e, rows_f = EARLY // ndp, LATE // ndp
    scratch = [
        pltpu.VMEM((1024, C), BF16), pltpu.VMEM((1, C), jnp.int32), pltpu.VMEM((3, C), F32),
        pltpu.VMEM((4, C, C), BF16), pltpu.VMEM((2, C, C), BF16),
        pltpu.VMEM((C, FFN), BF16), pltpu.VMEM((FFN, C), BF16),
        pltpu.SemaphoreType.DMA((7,)),
        pltpu.VMEM((C, C), F32),
        pltpu.VMEM((3, C, C), F32),
        pltpu.VMEM((4 * C, C), BF16),
        pltpu.VMEM((2, C, C), BF16),
        pltpu.VMEM((FFN, C), BF16),
        pltpu.VMEM((C, FFN), BF16),
        pltpu.VMEM((C, 5 * C), BF16),
        full, half, full, pltpu.VMEM((1, columns), F32), full, full, full, full,
        *([chunks] * 13),
        pltpu.VMEM((PEERS, 64, C), BF16),
        pltpu.VMEM((PEERS * PACK, C), F32), pltpu.VMEM((PEERS * PACK, C), F32), cube, cube,
        *([pltpu.VMEM((8, C, C), BF16)] * 3),
        half, big, half, half, big, full, pltpu.VMEM((5 * C, columns), BF16), half, half,
    ]
    scratch += [
        pltpu.VMEM((EARLY, C), BF16),
        pltpu.VMEM((EARLY // 2, C), BF16),
        pltpu.VMEM((EARLY // 2, C), BF16),
        pltpu.VMEM((ndp // 2, rows_e, C), BF16),
    ]
    for rows, whole in ((rows_e, EARLY), (rows_f, LATE)):
        if whole == LATE:
            scratch += [pltpu.VMEM((whole, C), BF16), pltpu.VMEM((ndp, rows, C), BF16)]
        scratch += [
            pltpu.VMEM((rows, C), BF16),
            pltpu.VMEM((PEERS, rows, C), BF16),
            pltpu.VMEM((rows, C), BF16),
            pltpu.VMEM((whole, C), BF16),
        ]
    scratch += [
        pltpu.SemaphoreType.DMA((6,)),
        pltpu.SemaphoreType.DMA((7, PIECES)),
        pltpu.SemaphoreType.DMA((4,)),
        pltpu.SemaphoreType.DMA((2,)),
        pltpu.SemaphoreType.DMA((8,)),
        pltpu.SemaphoreType.DMA((8,)),
    ]
    outs = tuple(
        jax.ShapeDtypeStruct(shape, BF16)
        for shape in ((1024, C), (1024, C), (4 * C, C), (2 * C, C), (C, FFN), (FFN, C), (3, C))
    )
    results = pl.pallas_call(
        functools.partial(kernel, ndp, scale),
        out_shape=outs,
        in_specs=[hbm] * 8,
        out_specs=(vmem,) * 7,
        scratch_shapes=scratch,
        compiler_params=pltpu.CompilerParams(
            collective_id=0, has_side_effects=True, vmem_limit_bytes=48 * 1024 * 1024
        ),
        cost_estimate=pl.CostEstimate(flops=1_600_000_000, bytes_accessed=3_000_000, transcendentals=1_200_000),
    )(
        *[
            pltpu.with_memory_space_constraint(array, pltpu.HBM)
            for array in (
                pair_repr.reshape(1024, C), cotangent.reshape(1024, C), residue_mask, norm_gains,
                w_proj, w_out, w_up, w_down,
            )
        ]
    )
    results = hand_over(outs, results)
    nxt, grad, g_proj, g_out, g_up, g_down, g_gains = results
    return (
        nxt.reshape(1, C, ROWS, C),
        grad.reshape(1, ROWS, C, C),
        g_proj.reshape(4, C, C),
        g_out.reshape(2, C, C),
        g_up,
        g_down,
        g_gains,
    )


def solution(mesh):
    in_specs = (
        P("dp", "dap", None, None),
        P("dp", None, "dap", None),
        P("dp", None),
        P(),
        P(),
        P(),
        P(),
        P(),
    )
    out_specs = (P("dp", None, "dap", None), P("dp", "dap", None, None), P(), P(), P(), P(), P())
    body = functools.partial(local, mesh.shape["dp"])
    return jax.shard_map(body, mesh=mesh, in_specs=in_specs, out_specs=out_specs, check_vma=False)
```

```python
import functools
import math

import jax
import jax.numpy as jnp
from jax import lax
from jax.experimental import pallas as pl
from jax.experimental.pallas import tpu as pltpu
from jax.sharding import PartitionSpec as P

EPSILON = 1e-05
GELU_SCALE = 0.7978845608028654
GELU_CUBIC = 0.044715
MESH = pl.DeviceIdType.MESH
F32 = jnp.float32
BF16 = jnp.bfloat16

C = 128
FFN = 512
ROWS = 8
PEERS = 16
PIECES = 4
PER = ROWS // PIECES
WIDE = PER * C
PACK = PER * 8
PART = PEERS * PER
EARLY = 1536
LATE = 512


AWAY = sorted(
    [(dy, dx) for dy in range(-3, 5) for dx in range(2) if dy or dx],
    key=lambda at: (-abs(at[0]) - 2 * at[1], at[0]),
)


def far_crops(ndp):
    depth = max(1, ndp // 4)
    steps = [(dz, dr) for dz in range(-((depth - 1) // 2), depth // 2 + 1) for dr in range(ndp // depth) if dz or dr]
    return sorted(steps, key=lambda at: (-abs(at[0]) - at[1] // 2, -at[1], at[0]))


def dot(left, right):
    return jnp.dot(left, right, preferred_element_type=F32)


def dot_nt(left, right):
    return lax.dot_general(left, right, (((1,), (1,)), ((), ())), preferred_element_type=F32)


def dot_tn(left, right):
    return lax.dot_general(left, right, (((0,), (0,)), ((), ())), preferred_element_type=F32)


def norm(values):
    average = jnp.sum(values, axis=0, keepdims=True) * (1.0 / C)
    centred = values - average
    inv_std = lax.rsqrt(jnp.sum(centred * centred, axis=0, keepdims=True) * (1.0 / C) + EPSILON)
    return centred * inv_std, inv_std


def norm_back(incoming, normed, inv_std, gain):
    scaled = incoming * gain
    first = jnp.sum(scaled, axis=0, keepdims=True) * (1.0 / C)
    second = jnp.sum(scaled * normed, axis=0, keepdims=True) * (1.0 / C)
    return inv_std * (scaled - first - normed * second)


def wide(block):
    return jnp.concatenate([block] * PER, axis=1) if PER > 1 else block


def split_rows(values):
    parts = [values[:, r * C:(r + 1) * C].reshape(PEERS, 8, C) for r in range(PER)]
    return jnp.concatenate(parts, axis=1) if PER > 1 else parts[0]


def join_rows(chunks):
    parts = [chunks[:, r * 8:(r + 1) * 8, :].reshape(C, C) for r in range(PER)]
    return jnp.concatenate(parts, axis=1) if PER > 1 else parts[0]


def kernel(
    ndp, scale,
    pair_h, cot, mask_h, gains_h, w_proj_h, w_out_h, w_up_h, w_down_h,
    out_next, out_grad, out_proj, out_out, out_up, out_down, out_gains,
    pair, mask_v, gains, w_proj, w_out, w_up, w_down, in_sem,
    held_g, mask_b, gain_b, wpT, woT, wuT, wdT, wcat,
    pairT, lnT, hat0, rstd0, ag, av, bg, bv,
    s_l, r_l, s_r, r_r, s_t, r_t, s_d, r_d, s_dl, r_dl, s_dr, r_dr, s_n, r_c,
    x_p, y_p, x_r, y_r, lc, rc, dc,
    tri_ln, hid, mid_b, mid_ln, d_pre, d_mid, d_stack, d_val, cotT,
    g_e, sib_e, half_e, rs_e, ch_e, ex_e, fin_e, ag_e, g_f, rs_f, ch_f, ex_f, fin_f, ag_f,
    send, recv, once, once_send, red, red_send,
):
    me = lax.axis_index("dap")
    my_dp = lax.axis_index("dp")
    barrier = pltpu.get_barrier_semaphore()

    def peer(dy, dx):
        return lax.rem(me // 2 + dy + 8, 8) * 2 + lax.rem(me + dx, 2)

    depth = max(1, ndp // 4)
    near = ndp // depth
    crops = far_crops(ndp)

    def crop(dz, dr):
        here = lax.rem(my_dp, near)
        if near == 4:
            there = lax.rem(here // 2 + dr // 2, 2) * 2 + lax.rem(here + dr, 2)
        else:
            there = lax.rem(here + dr, near)
        return lax.rem(my_dp // near + dz + depth, depth) * near + there

    for dy, dx in AWAY:
        pl.semaphore_signal(barrier, inc=1, device_id={"dap": peer(dy, dx)}, device_id_type=MESH)
    for dz, dr in crops:
        pl.semaphore_signal(barrier, inc=1, device_id={"dp": crop(dz, dr)}, device_id_type=MESH)

    loads = [
        pltpu.make_async_copy(src, dst, in_sem.at[n])
        for n, (src, dst) in enumerate((
            (pair_h, pair), (mask_h, mask_v), (gains_h, gains), (w_proj_h, w_proj),
            (w_out_h, w_out), (w_up_h, w_up), (w_down_h, w_down),
        ))
    ]
    for load in loads:
        load.start()
    for load in loads[1:4]:
        load.wait()

    mask_k = mask_v[...].astype(F32)
    mask_b[...] = jnp.broadcast_to(mask_k, (C, C)).T
    for n in range(3):
        gain_b[n] = jnp.broadcast_to(gains[n:n + 1, :], (C, C)).T
    for m in range(4):
        w_m = w_proj[m]
        wpT[m * C:(m + 1) * C, :] = w_m.astype(F32).T.astype(BF16)
        wcat[:, m * C:(m + 1) * C] = w_m
    loads[0].wait()

    def exchange(which, src, dst, p):
        for dy, dx in AWAY:
            d = peer(dy, dx)
            pltpu.make_async_remote_copy(
                src_ref=src.at[p, d], dst_ref=dst.at[p, me],
                send_sem=send.at[which], recv_sem=recv.at[which, p],
                device_id={"dap": d}, device_id_type=MESH,
            ).start()
        dst[p, me] = src[p, me]

    def arrived(which, dst, p):
        ref = dst.at[p, pl.ds(0, PEERS - 1)]
        pltpu.make_async_copy(ref, ref, recv.at[which, p]).wait()

    def sent(which, src):
        ref = src.at[:, pl.ds(0, PEERS - 1)]
        pltpu.make_async_copy(ref, ref, send.at[which]).wait()

    def mask_of(p):
        parts = []
        for r in range(PER):
            parts.append(mask_k * mask_b[pl.ds(me * ROWS + p * PER + r, 1), :])
        return jnp.concatenate(parts, axis=1) if PER > 1 else parts[0]

    def columns(p):
        return pl.ds(pl.multiple_of(p * WIDE, WIDE), WIDE)

    def front(p):
        at = columns(p)
        x_rows = pair[at, :].astype(F32)
        x = jnp.concatenate([x_rows[r * C:(r + 1) * C, :].T for r in range(PER)], axis=1) if PER > 1 else x_rows.T
        pairT[:, at] = x
        normed, inv_std = norm(x)
        hat0[:, at] = normed
        rstd0[:, at] = inv_std
        ln = (normed * wide(gain_b[0])).astype(BF16)
        lnT[:, at] = ln
        mask = mask_of(p)
        gate = jax.nn.sigmoid(dot(wpT[0:C, :], ln))
        value = dot(wpT[C:2 * C, :], ln)
        ag[:, at] = gate
        av[:, at] = value
        s_l[p] = split_rows(mask * gate * value).astype(BF16)
        gate = jax.nn.sigmoid(dot(wpT[2 * C:3 * C, :], ln))
        value = dot(wpT[3 * C:4 * C, :], ln)
        bg[:, at] = gate
        bv[:, at] = value
        s_r[p] = split_rows(mask * gate * value).astype(BF16)

    def front_step(p, _):
        exchange(1, s_r, r_r, p)
        front(p + 1)
        return 0

    def send_l(p, _):
        exchange(0, s_l, r_l, p)
        return 0

    front(0)
    pl.semaphore_wait(barrier, PEERS - 1 + ndp - 1)
    lax.fori_loop(0, PIECES - 1, front_step, 0)
    exchange(1, s_r, r_r, PIECES - 1)
    lax.fori_loop(0, PIECES, send_l, 0)

    own_cot = pltpu.make_async_copy(cot.at[pl.ds(pl.multiple_of(me * 64, 64), 64)], r_c.at[me], once.at[0])
    own_cot.start()

    def send_cot(p):
        here = pl.ds(pl.multiple_of(p * PACK, PACK), PACK)
        for dy, dx in AWAY:
            d = peer(dy, dx)
            pltpu.make_async_remote_copy(
                src_ref=cot.at[pl.ds(pl.multiple_of(d * 64 + p * PACK, PACK), PACK)], dst_ref=r_c.at[me, here],
                send_sem=once_send.at[0], recv_sem=recv.at[6, p],
                device_id={"dap": d}, device_id_type=MESH,
            ).start()

    for load in loads[4:]:
        load.wait()
    for m in range(4):
        f_at = slice(m * C, (m + 1) * C)
        wuT[f_at, :] = w_up[:, f_at].astype(F32).T.astype(BF16)
        wdT[:, f_at] = w_down[f_at, :].astype(F32).T.astype(BF16)
    for m in range(2):
        woT[m] = w_out[m].astype(F32).T.astype(BF16)
    wcat[:, 4 * C:5 * C] = w_out[0]
    g_e[1280:EARLY, :] = jnp.zeros((EARLY - 1280, C), BF16)

    def spread(dst, src, p):
        for s in range(PEERS):
            dst[pl.ds(pl.multiple_of(s * 64 + p * PACK, PACK), PACK), :] = src[p, s].astype(F32)

    def gather_chunks(p):
        return lambda ref: jnp.stack(
            [ref[pl.ds(pl.multiple_of(s * 64 + p * PACK, PACK), PACK), :] for s in range(PEERS)]
        ).astype(BF16)

    def take_r(p, _):
        arrived(1, r_r, p)
        spread(x_r, r_r, p)
        return 0

    lax.fori_loop(0, PIECES, take_r, 0)
    for c in range(8):
        rc[c] = x_r[pl.ds(c, C, 8), :].astype(BF16)

    def part(p):
        return pl.ds(pl.multiple_of(p * PART, PART), PART)

    def tri_step(p, _):
        arrived(0, r_l, p)
        x_p[0:PEERS * PACK, :] = r_l[p].astype(F32).reshape(PEERS * PACK, C)
        for c in range(8):
            left = x_p[pl.ds(c, PART, 8), :].astype(BF16)
            lc[c, part(p), :] = left
            y_p[pl.ds(c, PART, 8), :] = dot_nt(left, rc[c])
        s_t[p] = y_p[0:PEERS * PACK, :].reshape(PEERS, PACK, C).astype(BF16)
        exchange(2, s_t, r_t, p)
        send_cot(p)
        return 0

    lax.fori_loop(0, PIECES, tri_step, 0)

    own_cot.wait()

    def send_next(p, _):
        rows = pl.ds(pl.multiple_of(me * 64 + p * PACK, PACK), PACK)

        for dy, dx in AWAY:
            d = peer(dy, dx)
            pltpu.make_async_remote_copy(
                src_ref=s_n.at[p, d], dst_ref=out_next.at[rows],
                send_sem=once_send.at[1], recv_sem=once.at[2],
                device_id={"dap": d}, device_id_type=MESH,
            ).start()
        pltpu.make_async_copy(s_n.at[p, me], out_next.at[rows], once.at[3]).start()
        return 0

    def middle(p, _):
        at = columns(p)
        arrived(2, r_t, p)
        tri = join_rows(r_t[p].astype(F32))
        tri_hat, tri_rstd = norm(tri)
        t_ln = (tri_hat * wide(gain_b[1])).astype(BF16)
        tri_ln[:, at] = t_ln
        out_gate = jax.nn.sigmoid(dot(woT[0], lnT[:, at]))
        out_value = dot(woT[1], t_ln)
        mid_r = (pairT[:, at] + out_gate * out_value).astype(BF16)
        mid_b[:, at] = mid_r
        mid = mid_r.astype(F32)
        mid_hat, mid_rstd = norm(mid)
        m_ln = (mid_hat * wide(gain_b[2])).astype(BF16)
        mid_ln[:, at] = m_ln
        cot_piece = r_c.at[pl.ds(0, PEERS - 1), pl.ds(0, PACK)]
        pltpu.make_async_copy(cot_piece, cot_piece, recv.at[6, p]).wait()
        cot_rows = r_c[:, pl.ds(pl.multiple_of(p * PACK, PACK), PACK), :].astype(F32)
        cot_t = jnp.concatenate(
            [cot_rows[:, r * 8:(r + 1) * 8, :].reshape(C, C).T for r in range(PER)], axis=1
        )
        cot_b = cot_t.astype(BF16)
        cotT[:, at] = cot_b
        for f in range(4):
            f_at = slice(f * C, (f + 1) * C)
            u = dot(wuT[f_at, :], m_ln)
            square = u * u
            tanh = jnp.tanh(u * (GELU_SCALE + GELU_SCALE * GELU_CUBIC * square))
            half = 0.5 + 0.5 * tanh
            act = u * half
            slope = half + act * (1.0 - tanh) * (GELU_SCALE + 3.0 * GELU_SCALE * GELU_CUBIC * square)
            hid[f_at, at] = act.astype(BF16)
            d_pre[f_at, at] = (dot(w_down[f_at, :], cot_b) * slope).astype(BF16)
        d_mid_v = cot_t + norm_back(dot(w_up[...], d_pre[:, at]), mid_hat, mid_rstd, wide(gain_b[2]))
        d_mid[:, at] = d_mid_v
        d_gate = (d_mid_v * out_value * out_gate * (1.0 - out_gate)).astype(BF16)
        d_stack[4 * C:5 * C, at] = d_gate
        d_value = (d_mid_v * out_gate).astype(BF16)
        d_val[:, at] = d_value
        d_tri = norm_back(dot(w_out[1], d_value), tri_hat, tri_rstd, wide(gain_b[1]))
        s_d[p] = split_rows(d_tri).astype(BF16)
        exchange(3, s_d, r_d, p)
        return 0

    lax.fori_loop(0, PIECES, middle, 0)

    def make_next(p, _):
        at = columns(p)
        nxt = mid_b[:, at].astype(F32) + dot(wdT[...], hid[:, at])
        nxt_rows = jnp.concatenate(
            [nxt[:, r * C:(r + 1) * C].T.reshape(PEERS, 8, C) for r in range(PER)], axis=1
        )
        s_n[p] = nxt_rows.astype(BF16)
        return 0

    rows_e, rows_f = EARLY // ndp, LATE // ndp

    core = lax.rem(my_dp, 2)
    place_dp = my_dp // 2
    places = ndp // 2
    sibling = {"dp": place_dp * 2 + 1 - core}
    half_rows = EARLY // 2

    def core_half(which):
        return pl.ds(pl.multiple_of(which * half_rows, 16), half_rows)

    chips = [(dz, dr) for dz, dr in crops if dr % 2 == 0]

    def chip(dz, dr):
        return crop(dz, dr) // 2

    def spread_early():
        for dz, dr in chips:
            q = chip(dz, dr)
            pltpu.make_async_remote_copy(
                src_ref=half_e.at[pl.ds(pl.multiple_of(q * rows_e, 16), rows_e)], dst_ref=rs_e.at[place_dp],
                send_sem=red_send.at[0], recv_sem=red.at[0],
                device_id={"dp": q * 2 + core}, device_id_type=MESH,
            ).start()
        rs_e[place_dp] = half_e[pl.ds(pl.multiple_of(place_dp * rows_e, 16), rows_e), :]

    def gather_early():
        place = pl.ds(pl.multiple_of(core * half_rows + place_dp * rows_e, 16), rows_e)
        for dz, dr in chips:
            pltpu.make_async_remote_copy(
                src_ref=fin_e, dst_ref=ag_e.at[place],
                send_sem=red_send.at[4], recv_sem=red.at[4],
                device_id={"dp": chip(dz, dr) * 2 + core}, device_id_type=MESH,
            ).start()
        ag_e[place, :] = fin_e[...]

    def spread_late(side):
        target = 1 - side
        for dz, dr in chips:
            q = chip(dz, dr)
            pltpu.make_async_remote_copy(
                src_ref=g_f.at[pl.ds(pl.multiple_of(side * 2 * C + q * rows_f, 16), rows_f)], dst_ref=rs_f.at[my_dp],
                send_sem=red_send.at[2], recv_sem=red.at[2],
                device_id={"dp": q * 2 + target}, device_id_type=MESH,
            ).start()
        own = pl.ds(pl.multiple_of(side * 2 * C + place_dp * rows_f, 16), rows_f)

        @pl.when(core == target)
        def _():
            rs_f[my_dp] = g_f[own, :]

        @pl.when(core != target)
        def _():
            pltpu.make_async_remote_copy(
                src_ref=g_f.at[own], dst_ref=rs_f.at[my_dp],
                send_sem=red_send.at[2], recv_sem=red.at[2],
                device_id=sibling, device_id_type=MESH,
            ).start()

    def wait_count(ref, sem):
        pltpu.make_async_copy(ref, ref, sem).wait()

    def total(ref):
        return jnp.sum(ref[...].astype(F32), axis=0)

    def cross(which, src, dst):
        for dy, dx in AWAY:
            pltpu.make_async_remote_copy(
                src_ref=src, dst_ref=dst.at[me],
                send_sem=red_send.at[which], recv_sem=red.at[which],
                device_id={"dap": peer(dy, dx)}, device_id_type=MESH,
            ).start()
        dst[me] = src[...]

    def gather_late(which, src, dst, rows):
        place = pl.ds(pl.multiple_of((1 - core) * 2 * C + place_dp * rows, 16), rows)

        for dz, dr in crops:
            pltpu.make_async_remote_copy(
                src_ref=src, dst_ref=dst.at[place],
                send_sem=red_send.at[which], recv_sem=red.at[which],
                device_id={"dp": crop(dz, dr)}, device_id_type=MESH,
            ).start()
        dst[place, :] = src[...]

    for f in range(4):
        f_at = slice(f * C, (f + 1) * C)
        g_e[f_at, :] = dot_nt(mid_ln[...], d_pre[f_at, :]).astype(BF16)
        g_e[512 + f * C:512 + (f + 1) * C, :] = dot_nt(hid[f_at, :], cotT[...]).astype(BF16)
    g_e[1024:1152, :] = dot_nt(lnT[...], d_stack[4 * C:5 * C, :]).astype(BF16)
    g_e[1152:1280, :] = dot_nt(tri_ln[...], d_val[...]).astype(BF16)
    add_cores = pltpu.make_async_remote_copy(
        src_ref=g_e.at[core_half(1 - core)], dst_ref=sib_e,
        send_sem=red_send.at[1], recv_sem=red.at[6],
        device_id=sibling, device_id_type=MESH,
    )
    add_cores.start()

    def back_step(p, _):
        arrived(3, r_d, p)
        x_p[0:PEERS * PACK, :] = r_d[p].astype(F32).reshape(PEERS * PACK, C)
        for c in range(8):
            grad = x_p[pl.ds(c, PART, 8), :].astype(BF16)
            dc[c, part(p), :] = grad
            y_p[pl.ds(c, PART, 8), :] = dot(grad, rc[c])
        s_dl[p] = y_p[0:PEERS * PACK, :].reshape(PEERS, PACK, C).astype(BF16)
        exchange(4, s_dl, r_dl, p)
        return 0

    back_step(0, 0)
    add_cores.wait_recv()
    half_e[...] = (g_e[core_half(core), :].astype(F32) + sib_e[...].astype(F32)).astype(BF16)
    spread_early()
    lax.fori_loop(1, PIECES, back_step, 0)

    for c in range(8):
        y_r[pl.ds(c, C, 8), :] = dot_tn(dc[c], lc[c])

    def back_right(p, _):
        s_dr[p] = gather_chunks(p)(y_r)
        exchange(5, s_dr, r_dr, p)
        return 0

    lax.fori_loop(0, PIECES, back_right, 0)
    lax.fori_loop(0, PIECES, make_next, 0)

    def lower_left(p, _):
        at = columns(p)
        arrived(4, r_dl, p)
        grad = join_rows(r_dl[p].astype(F32)) * mask_of(p)
        gate = ag[:, at]
        with_gate = grad * gate
        d_stack[0:C, at] = (with_gate * av[:, at] * (1.0 - gate)).astype(BF16)
        d_stack[C:2 * C, at] = with_gate.astype(BF16)
        return 0

    def lower_right(p, _):
        at = columns(p)
        arrived(5, r_dr, p)
        grad = join_rows(r_dr[p].astype(F32)) * mask_of(p)
        gate = bg[:, at]
        with_gate = grad * gate
        d_stack[2 * C:3 * C, at] = (with_gate * bv[:, at] * (1.0 - gate)).astype(BF16)
        d_stack[3 * C:4 * C, at] = with_gate.astype(BF16)
        return 0

    lax.fori_loop(0, PIECES, lower_left, 0)
    for m in (0, 1):
        m_at = slice(m * C, (m + 1) * C)
        g_f[m_at, :] = dot_nt(lnT[...], d_stack[m_at, :]).astype(BF16)
    spread_late(0)
    wait_count(rs_e.at[pl.ds(0, places - 1)], red.at[0])
    ch_e[...] = total(rs_e).astype(BF16)
    cross(5, ch_e, ex_e)
    head = (PIECES - 1) * WIDE
    lax.fori_loop(0, PIECES - 1, lower_right, 0)
    for m in (2, 3):
        held_g[m - 2] = dot_nt(lnT[:, :head], d_stack[m * C:(m + 1) * C, :head])
    lower_right(PIECES - 1, 0)
    for m in (2, 3):
        m_at = slice(m * C, (m + 1) * C)
        g_f[m_at, :] = (held_g[m - 2] + dot_nt(lnT[:, head:], d_stack[m_at, head:])).astype(BF16)
    spread_late(1)

    def finish(p, _):
        at = columns(p)
        d_ln = dot(wcat[...], d_stack[:, at])
        result = d_mid[:, at] + norm_back(d_ln, hat0[:, at], rstd0[:, at], wide(gain_b[0]))
        for r in range(PER):
            row = pl.ds(pl.multiple_of(p * WIDE + r * C, C), C)
            out_grad[row, :] = result[:, r * C:(r + 1) * C].T.astype(BF16)
        return 0

    lax.fori_loop(0, PIECES, finish, 0)
    lax.fori_loop(0, PIECES, send_next, 0)

    wait_count(ex_e.at[pl.ds(0, PEERS - 1)], red.at[5])
    fin_e[...] = (total(ex_e) * scale).astype(BF16)
    gather_early()

    wait_count(rs_f.at[pl.ds(0, ndp - 1)], red.at[2])
    ch_f[...] = total(rs_f).astype(BF16)
    cross(3, ch_f, ex_f)
    wait_count(ex_f.at[pl.ds(0, PEERS - 1)], red.at[3])
    fin_f[...] = (total(ex_f) * scale).astype(BF16)
    gather_late(7, fin_f, ag_f, rows_f)

    wait_count(ag_e.at[pl.ds(0, (places - 1) * rows_e)], red.at[4])
    to_core = pltpu.make_async_remote_copy(
        src_ref=ag_e.at[core_half(core)], dst_ref=ag_e.at[core_half(core)],
        send_sem=red_send.at[6], recv_sem=red.at[1],
        device_id=sibling, device_id_type=MESH,
    )
    to_core.start()
    to_core.wait_recv()
    mid_sum = jnp.zeros((C, C), F32)
    for f in range(4):
        f_at = slice(f * C, (f + 1) * C)
        block = ag_e[f_at, :]
        out_up[:, f_at] = block
        mid_sum = mid_sum + block.astype(F32) * w_up[:, f_at].astype(F32)
    out_down[...] = ag_e[512:1024, :]
    out_out[...] = ag_e[1024:1280, :]
    pair_sum = ag_e[1024:1152, :].astype(F32) * w_out[0].astype(F32)
    tri_sum = ag_e[1152:1280, :].astype(F32) * w_out[1].astype(F32)

    wait_count(ag_f.at[pl.ds(0, (ndp - 1) * rows_f)], red.at[7])
    for m in range(4):
        block = ag_f[m * C:(m + 1) * C, :]
        pair_sum = pair_sum + block.astype(F32) * w_proj[m].astype(F32)
    out_proj[...] = ag_f[...]
    sums = [jnp.sum(s.T, axis=0, keepdims=True) for s in (pair_sum, tri_sum, mid_sum)]
    out_gains[...] = (jnp.concatenate(sums, axis=0) / gains[...]).astype(BF16)

    for which, src in enumerate((s_l, s_r, s_t, s_d, s_dl, s_dr)):
        sent(which, src)
    sent_cot = r_c.at[pl.ds(0, PEERS - 1)]
    wait_count(sent_cot, once_send.at[0])
    all_next = s_n.at[:, pl.ds(0, PEERS - 1)]
    wait_count(all_next, once_send.at[1])
    wait_count(all_next, once.at[2])
    wait_count(s_n.at[:, 0], once.at[3])
    add_cores.wait_send()
    to_core.wait_send()
    wait_count(rs_e.at[pl.ds(0, places - 1)], red_send.at[0])
    wait_count(ex_e.at[pl.ds(0, PEERS - 1)], red_send.at[5])
    wait_count(rs_f.at[pl.ds(0, ndp - 1)], red_send.at[2])
    wait_count(ex_f.at[pl.ds(0, PEERS - 1)], red_send.at[3])
    wait_count(ag_e.at[pl.ds(0, (places - 1) * rows_e)], red_send.at[4])
    wait_count(ag_f.at[pl.ds(0, (ndp - 1) * rows_f)], red_send.at[7])


def hand_over(outs, results):
    count = len(outs)

    def copies(*refs):
        sems = refs[2 * count]
        gives = [pltpu.make_async_copy(refs[n], refs[count + n], sems.at[n]) for n in range(count)]
        for give in gives:
            give.start()
        for give in gives:
            give.wait()

    return pl.pallas_call(
        copies,
        out_shape=outs,
        in_specs=[pl.BlockSpec(memory_space=pltpu.VMEM)] * count,
        out_specs=(pl.BlockSpec(memory_space=pltpu.HBM),) * count,
        scratch_shapes=[pltpu.SemaphoreType.DMA((count,))],
        compiler_params=pltpu.CompilerParams(vmem_limit_bytes=48 * 1024 * 1024),
        cost_estimate=pl.CostEstimate(flops=0, bytes_accessed=2_000_000, transcendentals=0),
    )(*results)


def local(ndp, pair_repr, cotangent, residue_mask, norm_gains, w_proj, w_out, w_up, w_down):
    scale = 1.0 / math.sqrt(ndp * C * C)
    hbm = pl.BlockSpec(memory_space=pltpu.HBM)
    vmem = pl.BlockSpec(memory_space=pltpu.VMEM)
    columns = ROWS * C
    chunks = pltpu.VMEM((PIECES, PEERS, PACK, C), BF16)
    full = pltpu.VMEM((C, columns), F32)
    half = pltpu.VMEM((C, columns), BF16)
    big = pltpu.VMEM((FFN, columns), BF16)
    cube = pltpu.VMEM((1024 + 8, C), F32)
    rows_e, rows_f = EARLY // ndp, LATE // ndp
    scratch = [
        pltpu.VMEM((1024, C), BF16), pltpu.VMEM((1, C), jnp.int32), pltpu.VMEM((3, C), F32),
        pltpu.VMEM((4, C, C), BF16), pltpu.VMEM((2, C, C), BF16),
        pltpu.VMEM((C, FFN), BF16), pltpu.VMEM((FFN, C), BF16),
        pltpu.SemaphoreType.DMA((7,)),
        pltpu.VMEM((2, C, C), F32),
        pltpu.VMEM((C, C), F32),
        pltpu.VMEM((3, C, C), F32),
        pltpu.VMEM((4 * C, C), BF16),
        pltpu.VMEM((2, C, C), BF16),
        pltpu.VMEM((FFN, C), BF16),
        pltpu.VMEM((C, FFN), BF16),
        pltpu.VMEM((C, 5 * C), BF16),
        full, half, full, pltpu.VMEM((1, columns), F32), full, full, full, full,
        *([chunks] * 13),
        pltpu.VMEM((PEERS, 64, C), BF16),
        pltpu.VMEM((PEERS * PACK + 8, C), F32), pltpu.VMEM((PEERS * PACK + 8, C), F32), cube, cube,
        *([pltpu.VMEM((8, C, C), BF16)] * 3),
        half, big, half, half, big, full, pltpu.VMEM((5 * C, columns), BF16), half, half,
    ]
    scratch += [
        pltpu.VMEM((EARLY, C), BF16),
        pltpu.VMEM((EARLY // 2, C), BF16),
        pltpu.VMEM((EARLY // 2, C), BF16),
        pltpu.VMEM((ndp // 2, rows_e, C), BF16),
    ]
    for rows, whole in ((rows_e, EARLY), (rows_f, LATE)):
        if whole == LATE:
            scratch += [pltpu.VMEM((whole, C), BF16), pltpu.VMEM((ndp, rows, C), BF16)]
        scratch += [
            pltpu.VMEM((rows, C), BF16),
            pltpu.VMEM((PEERS, rows, C), BF16),
            pltpu.VMEM((rows, C), BF16),
            pltpu.VMEM((whole, C), BF16),
        ]
    scratch += [
        pltpu.SemaphoreType.DMA((6,)),
        pltpu.SemaphoreType.DMA((7, PIECES)),
        pltpu.SemaphoreType.DMA((4,)),
        pltpu.SemaphoreType.DMA((2,)),
        pltpu.SemaphoreType.DMA((8,)),
        pltpu.SemaphoreType.DMA((8,)),
    ]
    outs = tuple(
        jax.ShapeDtypeStruct(shape, BF16)
        for shape in ((1024, C), (1024, C), (4 * C, C), (2 * C, C), (C, FFN), (FFN, C), (3, C))
    )
    results = pl.pallas_call(
        functools.partial(kernel, ndp, scale),
        out_shape=outs,
        in_specs=[hbm] * 8,
        out_specs=(vmem,) * 7,
        scratch_shapes=scratch,
        compiler_params=pltpu.CompilerParams(
            collective_id=0, has_side_effects=True, vmem_limit_bytes=48 * 1024 * 1024
        ),
        cost_estimate=pl.CostEstimate(flops=1_600_000_000, bytes_accessed=3_000_000, transcendentals=1_200_000),
    )(
        *[
            pltpu.with_memory_space_constraint(array, pltpu.HBM)
            for array in (
                pair_repr.reshape(1024, C), cotangent.reshape(1024, C), residue_mask, norm_gains,
                w_proj, w_out, w_up, w_down,
            )
        ]
    )
    results = hand_over(outs, results)
    nxt, grad, g_proj, g_out, g_up, g_down, g_gains = results
    return (
        nxt.reshape(1, C, ROWS, C),
        grad.reshape(1, ROWS, C, C),
        g_proj.reshape(4, C, C),
        g_out.reshape(2, C, C),
        g_up,
        g_down,
        g_gains,
    )


def solution(mesh):
    in_specs = (
        P("dp", "dap", None, None),
        P("dp", None, "dap", None),
        P("dp", None),
        P(),
        P(),
        P(),
        P(),
        P(),
    )
    out_specs = (P("dp", None, "dap", None), P("dp", "dap", None, None), P(), P(), P(), P(), P())
    body = functools.partial(local, mesh.shape["dp"])
    return jax.shard_map(body, mesh=mesh, in_specs=in_specs, out_specs=out_specs, check_vma=False)
```
